256 devices in a mesh: row: 16 (over y_lo, z), col: 16 (over x, y_hi, core).
Axes of the slice: x: 4, y: 4 (y_hi: 2, y_lo: 2; y = y_hi * 2 + y_lo), z: 8, core: 2. Of those that a mesh axis runs over, the one named last changes fastest.
Arguments:
- pair_rep: bfloat16 [512, 512, 128], P('row', 'col'), may hold values from -6 to 6
- residue_mask: int32 [512], replicated, may hold values 0 or 1
- input_weights: bfloat16 [2, 128, 512], replicated, may hold values from -0.5 to 0.5
- gate_weights: bfloat16 [2, 128, 128], replicated, may hold values from -0.5 to 0.5
- output_weights: bfloat16 [2, 128, 128], replicated, may hold values from -0.5 to 0.5
Outputs:
- updated_pair: bfloat16 [512, 512, 128], P('row', 'col')
The draws below stay inside these ranges and needn't reach their ends.
All inputs are finite; a program needn't handle non-finite values.
Results may differ from the reference program's by a relative error of at most 0.0095.
Values may be sent and summed in bfloat16 or wider, within the bound.
A program may use at most 128 MiB of HBM per device.

```python
import jax
import jax.numpy as jnp
from jax import lax

C = 128
CH = 128
RES = 512


def set_ends(entries, rng, low, largest):
    longest = entries.shape.index(max(entries.shape))
    spots = []
    for shift in (0, 1):
        where = [jax.random.randint(jax.random.fold_in(rng, axis), (), 0, length) for axis, length in enumerate(entries.shape)]
        where[longest] = (where[longest] + shift) % entries.shape[longest]
        spots.append(tuple(where))
    return entries.at[spots[0]].set(low).at[spots[1]].set(largest)


def level_of(key, shape, cuts, smallest, high):
    loudness = 1.0
    for axis_at, shards_of in cuts:
        heights = jax.random.uniform(jax.random.fold_in(jax.random.fold_in(key, 6), axis_at), (shards_of,), jnp.float32, smallest / len(cuts), high / len(cuts))
        loudness = loudness * jnp.repeat(jnp.exp(heights), shape[axis_at] // shards_of).reshape((-1,) + (1,) * (len(shape) - 1 - axis_at))
    return loudness


def centred(own_key, shape, spread, limit, shards=(), kind=jnp.bfloat16):
    result = spread * jax.random.normal(own_key, shape, jnp.float32)
    if shards:
        result = result * level_of(own_key, shape, shards, -0.22, 0.18)
    return jnp.clip(result, -limit, limit).astype(kind)


def setup_inputs(seed: int = 0) -> dict:
    key_of = jax.random.split(jax.random.key(seed), 6)
    pair_rep = centred(key_of[0], (RES, RES, C), 1.0, 6.0, ((0, 16), (1, 16)))
    residue_mask = set_ends((jax.random.randint(key_of[1], (RES,), 0, 8) < 7).astype(jnp.int32), jax.random.fold_in(key_of[1], 1), 0, 1)
    input_weights = centred(key_of[2], (2, C, 4 * CH), C ** -0.5, 0.5)
    gate_weights = centred(key_of[3], (2, C, C), C ** -0.5, 0.5)
    output_weights = centred(key_of[4], (2, CH, C), CH ** -0.5, 0.5)
    return {"pair_rep": pair_rep, "residue_mask": residue_mask, "input_weights": input_weights, "gate_weights": gate_weights, "output_weights": output_weights}


epsilon = 1e-05

def normalize(values):
    values = values.astype(jnp.float32)
    centered = values - lax.optimization_barrier(jnp.mean(values, axis=-1, keepdims=True))
    variance = lax.optimization_barrier(jnp.mean(centered * centered, axis=-1, keepdims=True))
    return centered * lax.rsqrt(variance + epsilon)

def project(pair_rep, pair_mask, input_weight, gate_weight):
    channels = pair_rep.shape[-1]
    hidden = input_weight.shape[1] // 4
    normed = normalize(pair_rep).astype(jnp.bfloat16).reshape(-1, channels)
    projected = jnp.dot(normed, input_weight, preferred_element_type=jnp.float32)
    masked = pair_mask.reshape(-1, 1)
    left_side = (jax.nn.sigmoid(projected[:, hidden:2 * hidden]) * projected[:, :hidden] * masked).astype(jnp.bfloat16)
    right_side = (jax.nn.sigmoid(projected[:, 3 * hidden:]) * projected[:, 2 * hidden:3 * hidden] * masked).astype(jnp.bfloat16)
    gate_value = jax.nn.sigmoid(jnp.dot(normed, gate_weight, preferred_element_type=jnp.float32))
    block_shape = (pair_rep.shape[0], pair_rep.shape[1], hidden)
    return (left_side.reshape(block_shape), right_side.reshape(block_shape), gate_value)

def finish(pair_rep, triangle, gate_value, output_weight):
    normed = normalize(triangle).astype(jnp.bfloat16).reshape(-1, triangle.shape[-1])
    update_term = gate_value * jnp.dot(normed, output_weight, preferred_element_type=jnp.float32)
    return (pair_rep.astype(jnp.float32) + update_term.reshape(pair_rep.shape)).astype(jnp.bfloat16)

def reference(pair_rep, residue_mask, input_weights, gate_weights, output_weights):
    validity = residue_mask.astype(jnp.float32)
    pair_mask = validity[:, None] * validity[None, :]
    left_side, right_side, gate_value = project(pair_rep, pair_mask, input_weights[0], gate_weights[0])
    triangle = jnp.einsum('ikc,jkc->ijc', left_side.astype(jnp.float32), right_side.astype(jnp.float32), precision=lax.Precision.HIGHEST)
    after_outgoing = finish(pair_rep, triangle, gate_value, output_weights[0])
    left_side, right_side, gate_value = project(after_outgoing, pair_mask, input_weights[1], gate_weights[1])
    triangle = jnp.einsum('kic,kjc->ijc', left_side.astype(jnp.float32), right_side.astype(jnp.float32), precision=lax.Precision.HIGHEST)
    return finish(after_outgoing, triangle, gate_value, output_weights[1])
```

```python
import functools

import jax
import jax.numpy as jnp
from jax import lax
from jax.experimental import pallas as pl
from jax.experimental.pallas import tpu as pltpu
from jax.sharding import PartitionSpec as P

EPS = 1e-05
MESH = pl.DeviceIdType.MESH
F32 = jnp.float32
BF16 = jnp.bfloat16


def sigmoid(x):
    return 0.5 * jnp.tanh(0.5 * x) + 0.5


def swap_blocks(parts):
    group = lax.broadcasted_iota(jnp.int32, parts[0].shape, parts[0].ndim - 1) // 32
    axis = parts[0].ndim - 1
    high = group >= 2
    odd = lax.rem(group, 2) == 1

    def far(a, b):
        c = pltpu.roll(jnp.where(high, a, b), 64, axis)
        return jnp.where(high, c, a), jnp.where(high, b, c)

    def near(a, b):
        c = jnp.where(odd, a, b)
        return jnp.where(odd, pltpu.roll(c, 32, axis), a), jnp.where(odd, b, pltpu.roll(c, 96, axis))

    p0, p2 = far(parts[0], parts[2])
    p1, p3 = far(parts[1], parts[3])
    p0, p1 = near(p0, p1)
    p2, p3 = near(p2, p3)
    return p0, p1, p2, p3


def kernel(
    z_ref, mask_ref, win_ref, wgate_ref, wout_ref, out_ref,
    zp, normed, wt, mask8, gate,
    send1, recv1, left0, right0, left1, right1, tri, send2, recv2, stage, fin,
    sem1s, sem1r, semxs, semxr, sem2s, sem2r, semfs, semfr, ready,
):
    r, c = lax.axis_index("row"), lax.axis_index("col")
    cc, core = c // 2, lax.rem(c, 2)
    me = r * 8 + cc
    sibling = (r, cc * 2 + 1 - core)

    barrier = pltpu.get_barrier_semaphore()

    @pl.loop(1, 16)
    def _(t):
        pl.semaphore_signal(barrier, inc=1, device_id=(lax.rem(r + t, 16), c), device_id_type=MESH)
        pl.semaphore_signal(barrier, inc=1, device_id=(r, lax.rem(c + t, 16)), device_id_type=MESH)

    valid = jnp.broadcast_to(mask_ref[...].astype(F32), (8, 512))
    n8 = lax.broadcasted_iota(jnp.int32, (8, 512), 1)
    t8 = lax.broadcasted_iota(jnp.int32, (8, 512), 0)
    n = lax.broadcasted_iota(jnp.int32, (512, 128), 0)
    l = lax.broadcasted_iota(jnp.int32, (512, 128), 1)
    rows = jnp.where(lax.rem(n8, 8) == t8, valid, 0.0).astype(BF16)
    pick_row = jnp.where(n // 8 == 4 * r + l // 32, 1.0, 0.0).astype(BF16)
    pick_col = jnp.where(n == 32 * c + lax.rem(l, 32), 1.0, 0.0).astype(BF16)
    mask8[...] = jnp.dot(rows, pick_row, preferred_element_type=F32) * jnp.dot(
        valid.astype(BF16), pick_col, preferred_element_type=F32
    )

    def normalize_rows(t, x):
        centred = x - jnp.mean(x, axis=-1, keepdims=True)
        variance = jnp.mean(centred * centred, axis=-1, keepdims=True)
        normed[pl.ds(t * 128, 128), :] = (centred * lax.rsqrt(variance + EPS)).astype(BF16)

    @pl.loop(0, 8)
    def _(t):
        for u in range(4):
            zp[pl.ds(t * 128 + u * 32, 32), :] = z_ref[pl.ds((u * 8 + t) * 32, 32), :]
        normalize_rows(t, zp[pl.ds(t * 128, 128), :].astype(F32))

    for u in range(2):
        for k in range(4):
            wt[u, k] = win_ref[u, :, k * 128 : (k + 1) * 128].astype(F32).T.astype(BF16)

    for update in range(2):
        half = r // 8 if update == 0 else c // 8
        slot = lax.rem(r, 8) * 16 + c if update == 0 else r * 8 + lax.rem(c, 8)
        own = half == core

        if update == 0:
            pl.semaphore_wait(barrier, 30)

            @pl.loop(1, 16)
            def _(t):
                pl.semaphore_signal(ready, inc=1, device_id=(r, lax.rem(c + t, 16)), device_id_type=MESH)

            pl.semaphore_wait(ready, 15)

        def send_one(row, chip, update=update, half=half, slot=slot):
            pltpu.make_async_remote_copy(
                src_ref=send1.at[update, row * 8 + chip],
                dst_ref=recv1.at[update, slot],
                send_sem=sem1s.at[update],
                recv_sem=sem1r.at[update],
                device_id=(row, chip * 2 + half),
                device_id_type=MESH,
            ).start()

        def project(step, carry, update=update, half=half, own=own, send_one=send_one):
            g = lax.rem(r // 2 + step, 8)
            at = pl.ds(pl.multiple_of(g * 16, 16), 16)
            w = jnp.concatenate([wt[update, k, at, :] for k in range(4)], axis=0)
            p = lax.dot_general(w, normed[...], (((1,), (1,)), ((), ())), preferred_element_type=F32)
            lhs = sigmoid(p[16:32]) * p[0:16]
            rhs = sigmoid(p[48:64]) * p[32:48]
            both = []
            for side in (lhs, rhs):
                tiles = jnp.stack([side[:, t * 128 : (t + 1) * 128] for t in range(8)], axis=0)
                both.append(jnp.swapaxes(tiles, 0, 1) * mask8[...][None])
            send1[update, at] = jnp.concatenate(both, axis=1).astype(BF16)
            for j in range(2):
                row = g * 2 + j

                def chips(d, carry, row=row):
                    send_one(row, lax.rem(cc + d, 8))
                    return carry

                lax.fori_loop(1, 8, chips, 0)

                @pl.when(row != r)
                def _(row=row):
                    send_one(row, cc)

                @pl.when((row == r) & jnp.logical_not(own))
                def _(row=row):
                    send_one(row, cc)

                @pl.when((row == r) & own)
                def _():
                    pltpu.make_async_copy(
                        send1.at[update, me], recv1.at[update, slot_of(update)], sem1r.at[update]
                    ).start()

            return carry

        def slot_of(update):
            return lax.rem(r, 8) * 16 + c if update == 0 else r * 8 + lax.rem(c, 8)

        lax.fori_loop(0, 8, project, 0)

        @pl.loop(0, 8)
        def _(t):
            x = normed[pl.ds(t * 128, 128), :]
            g = jnp.dot(x, wgate_ref[update], preferred_element_type=F32)
            gate[pl.ds(t * 128, 128), :] = sigmoid(g)

        pltpu.make_async_copy(recv1.at[update], recv1.at[update], sem1r.at[update]).wait()

        if update == 0:

            @pl.loop(0, 8)
            def _(i):
                x = recv1[0, pl.ds(i * 16, 16)].astype(F32).reshape(4, 4, 16, 128)
                parts = swap_blocks([x[:, q] for q in range(4)])
                for side, ref, base in ((0, left0, 0), (1, right0, core * 256)):
                    strip = jnp.concatenate(
                        [
                            jnp.concatenate([parts[u][k, side * 8 : side * 8 + 8] for k in range(4)], axis=1)
                            for u in range(4)
                        ],
                        axis=0,
                    )
                    ref[pl.ds(pl.multiple_of(base + i * 32, 32), 32), :] = strip.astype(BF16)

            mine = right0.at[pl.ds(pl.multiple_of(core * 256, 256), 256)]
            theirs = right0.at[pl.ds(pl.multiple_of((1 - core) * 256, 256), 256)]
        else:

            @pl.loop(0, 16)
            def _(i):
                x = recv1[1, pl.ds(i * 8, 8)].astype(F32).reshape(2, 4, 16, 128)
                parts = swap_blocks([x[:, q] for q in range(4)])
                for side in range(2):
                    strip = jnp.concatenate(
                        [
                            jnp.concatenate([parts[u][k, side * 8 : side * 8 + 8] for k in range(2)], axis=1)
                            for u in range(4)
                        ],
                        axis=0,
                    ).astype(BF16)
                    if side == 0:
                        left1[pl.ds(pl.multiple_of(i * 32, 32), 32), :] = strip
                    else:
                        right1[core, pl.ds(pl.multiple_of(i * 32, 32), 32), :] = strip

            mine = right1.at[core]
            theirs = right1.at[1 - core]
        give = pltpu.make_async_remote_copy(
            src_ref=mine, dst_ref=mine, send_sem=semxs.at[update], recv_sem=semxr.at[update],
            device_id=sibling, device_id_type=MESH,
        )
        give.start()
        pltpu.make_async_copy(theirs, theirs, semxr.at[update]).wait()

        if update == 0:
            tri[...] = lax.dot_general(
                left0[...], right0[...], (((1,), (1,)), ((), ())), preferred_element_type=F32
            )
        else:
            for h in range(2):
                tri[:, h * 256 : (h + 1) * 256] = lax.dot_general(
                    left1[...], right1[h], (((0,), (0,)), ((), ())), preferred_element_type=F32
                )

        to_core = r // 8
        origin = lax.rem(r, 8) * 8 + cc
        own_back = to_core == core

        def back(step, carry, update=update):
            b = lax.rem(lax.rem(r, 8) + step, 8)
            x = tri[pl.ds(pl.multiple_of(b * 32, 32), 32), :].reshape(4, 8, 512)
            parts = [jnp.stack([x[u, :, k * 128 : (k + 1) * 128] for k in range(4)], axis=0) for u in range(4)]
            parts = swap_blocks(parts)
            for y in range(2):
                pair = jnp.concatenate([parts[2 * y], parts[2 * y + 1]], axis=1).astype(BF16)
                for k in range(4):
                    send2[update, b * 8 + k * 2 + y] = pair[k]

            def one(chip):
                pltpu.make_async_remote_copy(
                    src_ref=send2.at[update, b * 8 + chip],
                    dst_ref=recv2.at[update, origin],
                    send_sem=sem2s.at[update],
                    recv_sem=sem2r.at[update],
                    device_id=(core * 8 + b, chip * 2 + to_core),
                    device_id_type=MESH,
                ).start()

            def chips(d, carry):
                one(lax.rem(cc + d, 8))
                return carry

            lax.fori_loop(1, 8, chips, 0)
            here = core * 8 + b == r

            @pl.when(jnp.logical_not(here))
            def _():
                one(cc)

            @pl.when(here)
            def _():
                pltpu.make_async_copy(
                    send2.at[update, b * 8 + cc], recv2.at[update, origin], sem2r.at[update]
                ).start()

            return carry

        lax.fori_loop(0, 8, back, 0)
        pltpu.make_async_copy(recv2.at[update], recv2.at[update], sem2r.at[update]).wait()

        x = jnp.swapaxes(recv2[update].astype(F32), 0, 1)
        first, second = x[0:8], x[8:16]
        low = core == 0
        fin[update, core] = jnp.where(low, first, second).astype(BF16)
        stage[update] = jnp.where(low, second, first).astype(BF16)
        cross = pltpu.make_async_remote_copy(
            src_ref=stage.at[update], dst_ref=fin.at[update, core],
            send_sem=semfs.at[update], recv_sem=semfr.at[update],
            device_id=sibling, device_id_type=MESH,
        )
        cross.start()
        other = fin.at[update, 1 - core]
        pltpu.make_async_copy(other, other, semfr.at[update]).wait()

        @pl.loop(0, 8)
        def _(t, update=update):
            x = jnp.concatenate([fin[update, 0, t], fin[update, 1, t]], axis=0).astype(F32)
            centred = x - jnp.mean(x, axis=0, keepdims=True)
            variance = jnp.mean(centred * centred, axis=0, keepdims=True)
            y = (centred * lax.rsqrt(variance + EPS)).astype(BF16)
            term = lax.dot_general(y, wout_ref[update], (((0,), (0,)), ((), ())), preferred_element_type=F32)
            at = pl.ds(pl.multiple_of(t * 128, 128), 128)
            z = (zp[at, :].astype(F32) + gate[at, :] * term).astype(BF16)
            if update == 0:
                zp[at, :] = z
                normalize_rows(t, z.astype(F32))
            else:
                for u in range(4):
                    out_ref[pl.ds(pl.multiple_of((u * 8 + t) * 32, 32), 32), :] = z[u * 32 : (u + 1) * 32]

        give.wait_send()
        cross.wait_send()

        @pl.when(own)
        def _(update=update):
            sent = send1.at[update, pl.ds(0, 127)]
            pltpu.make_async_copy(sent, sent, sem1s.at[update]).wait()

        @pl.when(jnp.logical_not(own))
        def _(update=update):
            sent = send1.at[update]
            pltpu.make_async_copy(sent, sent, sem1s.at[update]).wait()

        @pl.when(own_back)
        def _(update=update):
            sent = send2.at[update, pl.ds(0, 63)]
            pltpu.make_async_copy(sent, sent, sem2s.at[update]).wait()

        @pl.when(jnp.logical_not(own_back))
        def _(update=update):
            sent = send2.at[update]
            pltpu.make_async_copy(sent, sent, sem2s.at[update]).wait()


def per_device(pair_rep, residue_mask, input_weights, gate_weights, output_weights):
    vmem = pl.BlockSpec(memory_space=pltpu.VMEM)
    dma = pltpu.SemaphoreType.DMA((2,))
    out = pl.pallas_call(
        kernel,
        out_shape=jax.ShapeDtypeStruct((1024, 128), BF16),
        in_specs=[vmem] * 5,
        out_specs=vmem,
        scratch_shapes=[
            pltpu.VMEM((1024, 128), BF16),
            pltpu.VMEM((1024, 128), BF16),
            pltpu.VMEM((2, 4, 128, 128), BF16),
            pltpu.VMEM((8, 128), F32),
            pltpu.VMEM((1024, 128), F32),
            pltpu.VMEM((2, 128, 16, 128), BF16),
            pltpu.VMEM((2, 128, 16, 128), BF16),
            pltpu.VMEM((256, 512), BF16),
            pltpu.VMEM((512, 512), BF16),
            pltpu.VMEM((512, 256), BF16),
            pltpu.VMEM((2, 512, 256), BF16),
            pltpu.VMEM((256, 512), F32),
            pltpu.VMEM((2, 64, 16, 128), BF16),
            pltpu.VMEM((2, 64, 16, 128), BF16),
            pltpu.VMEM((2, 8, 64, 128), BF16),
            pltpu.VMEM((2, 2, 8, 64, 128), BF16),
            dma, dma, dma, dma, dma, dma, dma, dma,
            pltpu.SemaphoreType.REGULAR,
        ],
        compiler_params=pltpu.CompilerParams(
            collective_id=0, has_side_effects=True, vmem_limit_bytes=32 * 1024 * 1024
        ),
        name="triangles",
    )(
        pair_rep.reshape(1024, 128),
        residue_mask.reshape(1, 512),
        input_weights,
        gate_weights,
        output_weights,
    )
    return out.reshape(32, 32, 128)


def solution(mesh):
    placed = (P("row", "col", None), P(), P(), P(), P())
    return jax.shard_map(
        per_device, mesh=mesh, in_specs=placed, out_specs=P("row", "col", None), check_vma=False
    )
```

```python
import functools

import jax
import jax.numpy as jnp
from jax import lax
from jax.experimental import pallas as pl
from jax.experimental.pallas import tpu as pltpu
from jax.sharding import PartitionSpec as P

EPS = 1e-05
MESH = pl.DeviceIdType.MESH
F32 = jnp.float32
BF16 = jnp.bfloat16


def sigmoid(x):
    return 0.5 * jnp.tanh(0.5 * x) + 0.5


def swap_blocks(parts):
    group = lax.broadcasted_iota(jnp.int32, parts[0].shape, parts[0].ndim - 1) // 32
    axis = parts[0].ndim - 1
    high = group >= 2
    odd = lax.rem(group, 2) == 1

    def far(a, b):
        c = pltpu.roll(jnp.where(high, a, b), 64, axis)
        return jnp.where(high, c, a), jnp.where(high, b, c)

    def near(a, b):
        c = jnp.where(odd, a, b)
        return jnp.where(odd, pltpu.roll(c, 32, axis), a), jnp.where(odd, b, pltpu.roll(c, 96, axis))

    p0, p2 = far(parts[0], parts[2])
    p1, p3 = far(parts[1], parts[3])
    p0, p1 = near(p0, p1)
    p2, p3 = near(p2, p3)
    return p0, p1, p2, p3


def far_then_near(g):
    return 4 - g, jnp.where(g == 0, 0, 4 + g)


def kernel(
    z_hbm, mask_ref, win_hbm, wgate_hbm, wout_hbm, out_ref,
    zp, win, wgate, wout, normed, wt, mask8, gate,
    send1, recv1, left0, right0, left1, right1, tri, send2, recv2, stage, fin,
    load, sem1s, sem1r, semxs, semxr, sem2s, sem2r, semfs, semfr, ready,
):
    r, c = lax.axis_index("row"), lax.axis_index("col")
    cc, core = c // 2, lax.rem(c, 2)
    y, z = r // 8, lax.rem(r, 8)
    me = r * 8 + cc
    sibling = (r, cc * 2 + 1 - core)

    barrier = pltpu.get_barrier_semaphore()

    @pl.loop(1, 16)
    def _(t):
        pl.semaphore_signal(barrier, inc=1, device_id=(lax.rem(r + t, 16), c), device_id_type=MESH)
        pl.semaphore_signal(barrier, inc=1, device_id=(r, lax.rem(c + t, 16)), device_id_type=MESH)

    loads = [pltpu.make_async_copy(z_hbm.at[:, t], zp.at[t], load.at[t]) for t in range(8)]
    loads.append(pltpu.make_async_copy(win_hbm, win, load.at[8]))
    loads.append(pltpu.make_async_copy(wgate_hbm, wgate, load.at[9]))
    loads.append(pltpu.make_async_copy(wout_hbm, wout, load.at[10]))
    for one in loads:
        one.start()

    pl.semaphore_wait(barrier, 30)

    @pl.loop(1, 16)
    def _(t):
        pl.semaphore_signal(ready, inc=1, device_id=(r, lax.rem(c + t, 16)), device_id_type=MESH)

    valid = jnp.broadcast_to(mask_ref[...].astype(F32), (8, 512))
    n8 = lax.broadcasted_iota(jnp.int32, (8, 512), 1)
    t8 = lax.broadcasted_iota(jnp.int32, (8, 512), 0)
    n = lax.broadcasted_iota(jnp.int32, (512, 128), 0)
    l = lax.broadcasted_iota(jnp.int32, (512, 128), 1)
    rows = jnp.where(lax.rem(n8, 8) == t8, valid, 0.0).astype(BF16)
    pick_row = jnp.where(n // 8 == 4 * r + l // 32, 1.0, 0.0).astype(BF16)
    pick_col = jnp.where(n == 32 * c + lax.rem(l, 32), 1.0, 0.0).astype(BF16)
    mask8[...] = jnp.dot(rows, pick_row, preferred_element_type=F32) * jnp.dot(
        valid.astype(BF16), pick_col, preferred_element_type=F32
    )

    def normalize_rows(t, x):
        centred = x - jnp.mean(x, axis=-1, keepdims=True)
        variance = jnp.mean(centred * centred, axis=-1, keepdims=True)
        normed[pl.ds(t * 128, 128), :] = (centred * lax.rsqrt(variance + EPS)).astype(BF16)

    def turn_weights(u):
        w = win[u].astype(F32).T.reshape(4, 16, 8, 128)
        wt[u] = jnp.concatenate([w[k] for k in range(4)], axis=1).astype(BF16)

    for t in range(8):
        loads[t].wait()
        normalize_rows(t, zp[t].reshape(128, 128).astype(F32))
    loads[8].wait()
    turn_weights(0)

    for update in range(2):
        half = y if update == 0 else c // 8
        slot = z * 16 + c if update == 0 else r * 8 + lax.rem(c, 8)
        own = half == core
        if update == 0:
            pl.semaphore_wait(ready, 15)

        def project(step, carry, update=update, half=half, own=own, slot=slot):
            g = step // 2
            line = lax.rem(y + lax.rem(step, 2), 2) * 8
            near_far = [line + lax.rem(z + d, 8) for d in far_then_near(g)]
            w = jnp.concatenate([wt[update, row] for row in near_far], axis=0)
            p = lax.dot_general(w, normed[...], (((1,), (1,)), ((), ())), preferred_element_type=F32)
            for j, row in enumerate(near_far):
                both = []
                for k in (0, 16):
                    side = sigmoid(p[j * 32 + k + 8 : j * 32 + k + 16]) * p[j * 32 + k : j * 32 + k + 8]
                    tiles = jnp.stack([side[:, t * 128 : (t + 1) * 128] for t in range(8)], axis=0)
                    both.append(jnp.swapaxes(tiles, 0, 1) * mask8[...][None])
                send1[update, pl.ds(row * 8, 8)] = jnp.concatenate(both, axis=1).astype(BF16)

            def send(row, chip):
                pltpu.make_async_remote_copy(
                    src_ref=send1.at[update, row * 8 + chip],
                    dst_ref=recv1.at[update, slot],
                    send_sem=sem1s.at[update],
                    recv_sem=sem1r.at[update, g],
                    device_id=(row, chip * 2 + half),
                    device_id_type=MESH,
                ).start()

            here = (step == 0) & own
            send(near_far[0], cc)

            @pl.when(jnp.logical_not(here))
            def _():
                send(near_far[1], cc)

            @pl.when(here)
            def _():
                pltpu.make_async_copy(send1.at[update, me], recv1.at[update, slot], sem1r.at[update, g]).start()

            def chips(d, carry):
                chip = lax.rem(cc + d, 8)
                send(near_far[0], chip)
                send(near_far[1], chip)
                return carry

            lax.fori_loop(1, 8, chips, 0)
            return carry

        lax.fori_loop(0, 8, project, 0)

        if update == 0:
            turn_weights(1)
            loads[9].wait()
            loads[10].wait()

        @pl.loop(0, 4)
        def _(i, update=update):
            at = pl.ds(pl.multiple_of(i * 256, 256), 256)
            gate[at, :] = sigmoid(jnp.dot(normed[at, :], wgate[update], preferred_element_type=F32))

        width = 4 if update == 0 else 2
        left, right = (left0, right0) if update == 0 else (left1, right1)

        def strip(i, at, update=update, width=width, left=left, right=right):
            x = recv1[update, pl.ds(i * width * 4, width * 4)].astype(F32).reshape(width, 4, 16, 128)
            parts = swap_blocks([x[:, q] for q in range(4)])
            for side in range(2):
                rows = [
                    jnp.concatenate([parts[u][k, side * 8 : side * 8 + 8] for k in range(width)], axis=1)
                    for u in range(4)
                ]
                rows = jnp.concatenate(rows, axis=0).astype(BF16)
                if side == 0:
                    left[at, :] = rows
                else:
                    right[core, at, :] = rows
            part = right.at[core, at]
            pltpu.make_async_remote_copy(
                src_ref=part, dst_ref=part, send_sem=semxs.at[update], recv_sem=semxr.at[update],
                device_id=sibling, device_id_type=MESH,
            ).start()

        def arrive(g, carry, update=update, strip=strip):
            got = recv1.at[update, pl.ds(0, 32)]
            pltpu.make_async_copy(got, got, sem1r.at[update, g]).wait()
            for d in far_then_near(g):
                source = lax.rem(z + 8 - d, 8)
                for line in (0, 8)[: update + 1]:
                    i = source + line
                    strip(i, pl.ds(pl.multiple_of(i * 32, 32), 32))
            return carry

        lax.fori_loop(0, 4, arrive, 0)

        contract = 1 if update == 0 else 0

        def product(h, update=update, contract=contract, left=left, right=right):
            tri[h] = lax.dot_general(
                left[...], right[h], (((contract,), (contract,)), ((), ())), preferred_element_type=F32
            )

        product(core)
        theirs = right.at[1 - core]
        pltpu.make_async_copy(theirs, theirs, semxr.at[update]).wait()
        product(1 - core)

        origin = z * 8 + cc
        own_back = y == core

        def back(g, carry, update=update):
            blocks = [lax.rem(z + d, 8) for d in far_then_near(g)]
            for b in blocks:
                parts = []
                for u in range(4):
                    x = tri[:, pl.ds(pl.multiple_of(b * 32 + u * 8, 8), 8), :]
                    parts.append(jnp.stack([x[k // 2, :, k % 2 * 128 : k % 2 * 128 + 128] for k in range(4)], axis=0))
                parts = swap_blocks(parts)
                for s in range(2):
                    pair = jnp.concatenate([parts[2 * s], parts[2 * s + 1]], axis=1).astype(BF16)
                    for k in range(4):
                        send2[update, b * 8 + k * 2 + s] = pair[k]

            def send(b, chip):
                pltpu.make_async_remote_copy(
                    src_ref=send2.at[update, b * 8 + chip],
                    dst_ref=recv2.at[update, origin],
                    send_sem=sem2s.at[update],
                    recv_sem=sem2r.at[update],
                    device_id=(core * 8 + b, chip * 2 + y),
                    device_id_type=MESH,
                ).start()

            here = (g == 0) & own_back
            send(blocks[0], cc)

            @pl.when(jnp.logical_not(here))
            def _():
                send(blocks[1], cc)

            @pl.when(here)
            def _():
                pltpu.make_async_copy(
                    send2.at[update, z * 8 + cc], recv2.at[update, origin], sem2r.at[update]
                ).start()

            def chips(d, carry):
                chip = lax.rem(cc + d, 8)
                send(blocks[0], chip)
                send(blocks[1], chip)
                return carry

            lax.fori_loop(1, 8, chips, 0)
            return carry

        lax.fori_loop(0, 4, back, 0)
        pltpu.make_async_copy(recv2.at[update], recv2.at[update], sem2r.at[update]).wait()

        x = jnp.swapaxes(recv2[update].astype(F32), 0, 1)
        first, second = x[0:8], x[8:16]
        low = core == 0
        stage[update] = jnp.where(low, second, first).astype(BF16)
        cross = pltpu.make_async_remote_copy(
            src_ref=stage.at[update], dst_ref=fin.at[update, core],
            send_sem=semfs.at[update], recv_sem=semfr.at[update],
            device_id=sibling, device_id_type=MESH,
        )
        cross.start()
        fin[update, core] = jnp.where(low, first, second).astype(BF16)
        other = fin.at[update, 1 - core]
        pltpu.make_async_copy(other, other, semfr.at[update]).wait()

        def finish(t, carry, update=update):
            x = jnp.concatenate([fin[update, 0, t], fin[update, 1, t]], axis=0).astype(F32)
            centred = x - jnp.mean(x, axis=0, keepdims=True)
            variance = jnp.mean(centred * centred, axis=0, keepdims=True)
            x = (centred * lax.rsqrt(variance + EPS)).astype(BF16)
            term = lax.dot_general(x, wout[update], (((0,), (0,)), ((), ())), preferred_element_type=F32)
            at = pl.ds(pl.multiple_of(t * 128, 128), 128)
            new = (zp[t].reshape(128, 128).astype(F32) + gate[at, :] * term).astype(BF16)
            if update == 0:
                zp[t] = new.reshape(4, 32, 128)
                normalize_rows(t, new.astype(F32))
            else:
                out_ref[:, t] = new.reshape(4, 32, 128)
            return carry

        lax.fori_loop(0, 8, finish, 0, unroll=4)

        mine = right.at[core]
        pltpu.make_async_copy(mine, mine, semxs.at[update]).wait()
        cross.wait_send()
        for sent, sem, all_remote, count in (
            (send1, sem1s, jnp.logical_not(own), 128),
            (send2, sem2s, jnp.logical_not(own_back), 64),
        ):

            @pl.when(all_remote)
            def _(update=update, sent=sent, sem=sem):
                pltpu.make_async_copy(sent.at[update], sent.at[update], sem.at[update]).wait()

            @pl.when(jnp.logical_not(all_remote))
            def _(update=update, sent=sent, sem=sem, count=count):
                gone = sent.at[update, pl.ds(0, count - 1)]
                pltpu.make_async_copy(gone, gone, sem.at[update]).wait()


def per_device(pair_rep, residue_mask, input_weights, gate_weights, output_weights):
    vmem = pl.BlockSpec(memory_space=pltpu.VMEM)
    anywhere = pl.BlockSpec(memory_space=pl.ANY)
    dma = pltpu.SemaphoreType.DMA((2,))
    out = pl.pallas_call(
        kernel,
        out_shape=jax.ShapeDtypeStruct((4, 8, 32, 128), BF16),
        in_specs=[anywhere, vmem, anywhere, anywhere, anywhere],
        out_specs=vmem,
        scratch_shapes=[
            pltpu.VMEM((8, 4, 32, 128), BF16),
            pltpu.VMEM((2, 128, 512), BF16),
            pltpu.VMEM((2, 128, 128), BF16),
            pltpu.VMEM((2, 128, 128), BF16),
            pltpu.VMEM((1024, 128), BF16),
            pltpu.VMEM((2, 16, 32, 128), BF16),
            pltpu.VMEM((8, 128), F32),
            pltpu.VMEM((1024, 128), F32),
            pltpu.VMEM((2, 128, 16, 128), BF16),
            pltpu.VMEM((2, 128, 16, 128), BF16),
            pltpu.VMEM((256, 512), BF16),
            pltpu.VMEM((2, 256, 512), BF16),
            pltpu.VMEM((512, 256), BF16),
            pltpu.VMEM((2, 512, 256), BF16),
            pltpu.VMEM((2, 256, 256), F32),
            pltpu.VMEM((2, 64, 16, 128), BF16),
            pltpu.VMEM((2, 64, 16, 128), BF16),
            pltpu.VMEM((2, 8, 64, 128), BF16),
            pltpu.VMEM((2, 2, 8, 64, 128), BF16),
            pltpu.SemaphoreType.DMA((11,)),
            dma, pltpu.SemaphoreType.DMA((2, 4)), dma, dma, dma, dma, dma, dma,
            pltpu.SemaphoreType.REGULAR,
        ],
        compiler_params=pltpu.CompilerParams(
            collective_id=0, has_side_effects=True, vmem_limit_bytes=56 * 1024 * 1024
        ),
        name="triangles",
    )(
        pair_rep.reshape(4, 8, 32, 128),
        residue_mask.reshape(1, 512),
        input_weights,
        gate_weights,
        output_weights,
    )
    return out.reshape(32, 32, 128)


def solution(mesh):
    placed = (P("row", "col", None), P(), P(), P(), P())
    return jax.shard_map(
        per_device, mesh=mesh, in_specs=placed, out_specs=P("row", "col", None), check_vma=False
    )
```

```python
import functools

import jax
import jax.numpy as jnp
from jax import lax
from jax.experimental import pallas as pl
from jax.experimental.pallas import tpu as pltpu
from jax.sharding import PartitionSpec as P

EPS = 1e-05
MESH = pl.DeviceIdType.MESH
F32 = jnp.float32
BF16 = jnp.bfloat16


def sigmoid(x):
    return 0.5 * jnp.tanh(0.5 * x) + 0.5


def swap_blocks(parts):
    group = lax.broadcasted_iota(jnp.int32, parts[0].shape, parts[0].ndim - 1) // 32
    axis = parts[0].ndim - 1
    high = group >= 2
    odd = lax.rem(group, 2) == 1

    def far(a, b):
        c = pltpu.roll(jnp.where(high, a, b), 64, axis)
        return jnp.where(high, c, a), jnp.where(high, b, c)

    def near(a, b):
        c = jnp.where(odd, a, b)
        return jnp.where(odd, pltpu.roll(c, 32, axis), a), jnp.where(odd, b, pltpu.roll(c, 96, axis))

    p0, p2 = far(parts[0], parts[2])
    p1, p3 = far(parts[1], parts[3])
    p0, p1 = near(p0, p1)
    p2, p3 = near(p2, p3)
    return p0, p1, p2, p3


def far_first(step):
    pair, second = step // 2, lax.rem(step, 2)
    middle = (pair == 1) | (pair == 2)
    dx = jnp.where(middle, 1 + 2 * second, jnp.where(pair == 0, 2, 0))
    return dx, jnp.where(middle, 2 - pair, 1 - second)


ALONG_Z = (4, 3, 5, 2, 6, 1, 7, 0)


def kernel(
    z_hbm, mask_ref, win_hbm, wgate_hbm, wout_hbm, out_ref,
    zp, win, wgate, wout, wfin, normed, wt, mask8, gate,
    send1, recv1, left0, right0, left1, right1, send2, recv2, stage, fin,
    load, sem1s, sem1r, semxs, semxr, sem2s, sem2r, semfs, semfr, ready,
):
    r, c = lax.axis_index("row"), lax.axis_index("col")
    cc, core = c // 2, lax.rem(c, 2)
    y, z = r // 8, lax.rem(r, 8)
    x, yh = cc // 2, lax.rem(cc, 2)
    me = cc * 16 + r
    sibling = (r, cc * 2 + 1 - core)

    barrier = pltpu.get_barrier_semaphore()

    @pl.loop(1, 16)
    def _(t):
        pl.semaphore_signal(barrier, inc=1, device_id=(lax.rem(r + t, 16), c), device_id_type=MESH)
        pl.semaphore_signal(barrier, inc=1, device_id=(r, lax.rem(c + t, 16)), device_id_type=MESH)

    loads = [pltpu.make_async_copy(z_hbm.at[:, t], zp.at[t], load.at[t]) for t in range(8)]
    loads.append(pltpu.make_async_copy(win_hbm, win, load.at[8]))
    loads.append(pltpu.make_async_copy(wgate_hbm, wgate, load.at[9]))
    loads.append(pltpu.make_async_copy(wout_hbm, wout, load.at[10]))
    for one in loads:
        one.start()

    pl.semaphore_wait(barrier, 30)

    @pl.loop(1, 16)
    def _(t):
        pl.semaphore_signal(ready, inc=1, device_id=(r, lax.rem(c + t, 16)), device_id_type=MESH)

    valid = jnp.broadcast_to(mask_ref[...].astype(F32), (8, 512))
    n8 = lax.broadcasted_iota(jnp.int32, (8, 512), 1)
    t8 = lax.broadcasted_iota(jnp.int32, (8, 512), 0)
    n = lax.broadcasted_iota(jnp.int32, (512, 128), 0)
    l = lax.broadcasted_iota(jnp.int32, (512, 128), 1)
    rows = jnp.where(lax.rem(n8, 8) == t8, valid, 0.0).astype(BF16)
    pick_row = jnp.where(n // 8 == 4 * r + l // 32, 1.0, 0.0).astype(BF16)
    pick_col = jnp.where(n == 32 * c + lax.rem(l, 32), 1.0, 0.0).astype(BF16)
    mask8[...] = jnp.dot(rows, pick_row, preferred_element_type=F32) * jnp.dot(
        valid.astype(BF16), pick_col, preferred_element_type=F32
    )

    def normalize_rows(t, v):
        centred = v - jnp.mean(v, axis=-1, keepdims=True)
        variance = jnp.mean(centred * centred, axis=-1, keepdims=True)
        normed[pl.ds(t * 128, 128), :] = (centred * lax.rsqrt(variance + EPS)).astype(BF16)

    def turn_weights(u):
        for k in range(4):
            wt[u, k] = win[u, :, k * 128 : (k + 1) * 128].astype(F32).T.astype(BF16)

    def project(step, update):
        dx, dh = far_first(step)
        chip = lax.rem(x + dx, 4) * 2 + lax.rem(yh + dh, 2)
        at = pl.ds(pl.multiple_of(chip * 16, 16), 16)
        w = jnp.concatenate([wt[update, k, at, :] for k in range(4)], axis=0)
        p = lax.dot_general(w, normed[...], (((1,), (1,)), ((), ())), preferred_element_type=F32)
        both = []
        for k in (0, 32):
            side = sigmoid(p[k + 16 : k + 32]) * p[k : k + 16]
            tiles = jnp.stack([side[:, t * 128 : (t + 1) * 128] for t in range(8)], axis=0)
            both.append(jnp.swapaxes(tiles, 0, 1) * mask8[...][None])
        send1[update, at] = jnp.concatenate(both, axis=1).astype(BF16)

    for t in range(8):
        loads[t].wait()
        normalize_rows(t, zp[t].reshape(128, 128).astype(F32))
    loads[8].wait()
    turn_weights(0)

    for update in range(2):
        half = y if update == 0 else c // 8
        corner = lax.rem(c, 4)
        slot = x * 32 + z * 4 + corner if update == 0 else lax.rem(x, 2) * 64 + r * 4 + corner
        own = half == core
        if update == 0:

            @pl.loop(0, 8)
            def _(step):
                project(step, 0)

            pl.semaphore_wait(ready, 15)

        def spread(step, carry, update=update, half=half, own=own, slot=slot):
            if update == 1:
                project(step, 1)
            dx, dh = far_first(step)
            chip = lax.rem(x + dx, 4) * 2 + lax.rem(yh + dh, 2)

            def send(row):
                pltpu.make_async_remote_copy(
                    src_ref=send1.at[update, chip * 16 + row],
                    dst_ref=recv1.at[update, slot],
                    send_sem=sem1s.at[update],
                    recv_sem=sem1r.at[update, dx],
                    device_id=(row, chip * 2 + half),
                    device_id_type=MESH,
                ).start()

            far, near = lax.rem(y + 1 - dh, 2) * 8, lax.rem(y + dh, 2) * 8
            for line in (far, near):
                for dz in ALONG_Z[:-1]:
                    send(line + lax.rem(z + dz, 8))
                if line is far:
                    send(line + z)
            here = (step == 7) & own

            @pl.when(jnp.logical_not(here))
            def _():
                send(near + z)

            @pl.when(here)
            def _():
                pltpu.make_async_copy(send1.at[update, me], recv1.at[update, slot], sem1r.at[update, dx]).start()

            return carry

        lax.fori_loop(0, 8, spread, 0)

        if update == 0:
            turn_weights(1)
            loads[9].wait()
            loads[10].wait()
            for u in range(2):
                w = wout[u].astype(F32).reshape(8, 2, 8, 128)
                wfin[u] = jnp.concatenate([w[:, k].reshape(64, 128) for k in range(2)], axis=0).astype(BF16)

        @pl.loop(0, 4)
        def _(i, update=update):
            at = pl.ds(pl.multiple_of(i * 256, 256), 256)
            gate[at, :] = sigmoid(jnp.dot(normed[at, :], wgate[update], preferred_element_type=F32))

        left, right = (left0, right0) if update == 0 else (left1, right1)
        columns = 4 if update == 0 else 2
        count = 128 // columns

        def arrive(dx, update=update, left=left, right=right, columns=columns, count=count):
            k = lax.rem(x + 4 - dx, columns)
            got = recv1.at[update, pl.ds(0, count)]
            pltpu.make_async_copy(got, got, sem1r.at[update, dx]).wait()
            for part in range(count // 32):
                at = pl.ds(part * 256, 256)
                v = recv1[update, pl.ds(k * count + part * 32, 32)].astype(F32).reshape(8, 4, 16, 128)
                parts = swap_blocks([v[:, q] for q in range(4)])
                for side in range(2):
                    rows = jnp.stack([p[:, side * 8 : side * 8 + 8] for p in parts], axis=1)
                    rows = rows.reshape(256, 128).astype(BF16)
                    if side == 0:
                        left[k, at, :] = rows
                    else:
                        right[core, k, at, :] = rows
            part = right.at[core, k]
            pltpu.make_async_remote_copy(
                src_ref=part, dst_ref=part, send_sem=semxs.at[update], recv_sem=semxr.at[update],
                device_id=sibling, device_id_type=MESH,
            ).start()

        if update == 0:

            def each(i, carry, arrive=arrive):
                arrive(jnp.where(i == 0, 2, jnp.where(i == 3, 0, 2 * i - 1)))
                return carry

            lax.fori_loop(0, 4, each, 0)
        else:
            ways = lax.rem(x + 4 - core * 2, 4)
            other = lax.rem(ways + 3, 4)
            even, odd = jnp.where(lax.rem(ways, 2) == 0, ways, other), jnp.where(lax.rem(ways, 2) == 0, other, ways)
            arrive(jnp.where(even == 2, even, odd))
            arrive(jnp.where(even == 2, odd, even))
        theirs = right.at[1 - core]
        pltpu.make_async_copy(theirs, theirs, semxr.at[update]).wait()

        origin = cc * 8 + z
        own_back = y == core

        def back(i, carry, update=update, left=left, right=right):
            dx = jnp.where(i == 0, 2, jnp.where(i == 3, 0, 2 * i - 1))
            k = lax.rem(x + dx, 4)
            if update == 0:
                some = pl.ds(pl.multiple_of(lax.rem(k, 2) * 128, 128), 128)
                lhs = jnp.concatenate([left[q] for q in range(4)], axis=1)
                rhs = jnp.concatenate([right[k // 2, q, some, :] for q in range(4)], axis=1)
                v = lax.dot_general(lhs, rhs, (((1,), (1,)), ((), ())), preferred_element_type=F32)
            else:
                lhs = jnp.concatenate([left[q] for q in range(2)], axis=1)
                rhs = right[k // 2, lax.rem(k, 2)]
                v = lax.dot_general(lhs, rhs, (((0,), (0,)), ((), ())), preferred_element_type=F32)
            v = v.reshape(8, 4, 8, 128)
            parts = swap_blocks([v[:, u] for u in range(4)])
            for h in range(2):
                pair = jnp.concatenate([parts[2 * h], parts[2 * h + 1]], axis=1).astype(BF16)
                send2[update, pl.ds((k * 2 + h) * 8, 8)] = pair

            def send(chip, b):
                pltpu.make_async_remote_copy(
                    src_ref=send2.at[update, chip * 8 + b],
                    dst_ref=recv2.at[update, origin],
                    send_sem=sem2s.at[update],
                    recv_sem=sem2r.at[update],
                    device_id=(core * 8 + b, chip * 2 + y),
                    device_id_type=MESH,
                ).start()

            far, near = k * 2 + 1 - yh, k * 2 + yh
            for chip in (far, near):
                for dz in ALONG_Z[:-1]:
                    send(chip, lax.rem(z + dz, 8))
                if chip is far:
                    send(chip, z)
            here = (i == 3) & own_back

            @pl.when(jnp.logical_not(here))
            def _():
                send(near, z)

            @pl.when(here)
            def _():
                pltpu.make_async_copy(
                    send2.at[update, cc * 8 + z], recv2.at[update, origin], sem2r.at[update]
                ).start()

            return carry

        lax.fori_loop(0, 4, back, 0)
        pltpu.make_async_copy(recv2.at[update], recv2.at[update], sem2r.at[update]).wait()

        v = jnp.swapaxes(recv2[update].astype(F32), 0, 1)
        first, second = v[0:8], v[8:16]
        low = core == 0
        stage[update] = jnp.where(low, second, first).astype(BF16)
        cross = pltpu.make_async_remote_copy(
            src_ref=stage.at[update], dst_ref=fin.at[update, core],
            send_sem=semfs.at[update], recv_sem=semfr.at[update],
            device_id=sibling, device_id_type=MESH,
        )
        cross.start()
        fin[update, core] = jnp.where(low, first, second).astype(BF16)
        other = fin.at[update, 1 - core]
        pltpu.make_async_copy(other, other, semfr.at[update]).wait()

        def finish(t, carry, update=update):
            v = jnp.concatenate([fin[update, 0, t], fin[update, 1, t]], axis=0).astype(F32)
            centred = v - jnp.mean(v, axis=0, keepdims=True)
            variance = jnp.mean(centred * centred, axis=0, keepdims=True)
            v = (centred * lax.rsqrt(variance + EPS)).astype(BF16)
            term = lax.dot_general(v, wfin[update], (((0,), (0,)), ((), ())), preferred_element_type=F32)
            at = pl.ds(pl.multiple_of(t * 128, 128), 128)
            new = (zp[t].reshape(128, 128).astype(F32) + gate[at, :] * term).astype(BF16)
            if update == 0:
                zp[t] = new.reshape(4, 32, 128)
                normalize_rows(t, new.astype(F32))
            else:
                for u in range(4):
                    out_ref[u * 8 + t] = new[u * 32 : u * 32 + 32]
            return carry

        lax.fori_loop(0, 8, finish, 0, unroll=8)

        mine = right.at[core]
        pltpu.make_async_copy(mine, mine, semxs.at[update]).wait()
        cross.wait_send()
        for sent, sem, all_remote, count in (
            (send1, sem1s, jnp.logical_not(own), 128),
            (send2, sem2s, jnp.logical_not(own_back), 64),
        ):

            @pl.when(all_remote)
            def _(update=update, sent=sent, sem=sem):
                pltpu.make_async_copy(sent.at[update], sent.at[update], sem.at[update]).wait()

            @pl.when(jnp.logical_not(all_remote))
            def _(update=update, sent=sent, sem=sem, count=count):
                gone = sent.at[update, pl.ds(0, count - 1)]
                pltpu.make_async_copy(gone, gone, sem.at[update]).wait()


def per_device(pair_rep, residue_mask, input_weights, gate_weights, output_weights):
    vmem = pl.BlockSpec(memory_space=pltpu.VMEM)
    anywhere = pl.BlockSpec(memory_space=pl.ANY)
    dma = pltpu.SemaphoreType.DMA((2,))
    out = pl.pallas_call(
        kernel,
        out_shape=jax.ShapeDtypeStruct((32, 32, 128), BF16),
        in_specs=[anywhere, vmem, anywhere, anywhere, anywhere],
        out_specs=vmem,
        scratch_shapes=[
            pltpu.VMEM((8, 4, 32, 128), BF16),
            pltpu.VMEM((2, 128, 512), BF16),
            pltpu.VMEM((2, 128, 128), BF16),
            pltpu.VMEM((2, 128, 128), BF16),
            pltpu.VMEM((2, 128, 128), BF16),
            pltpu.VMEM((1024, 128), BF16),
            pltpu.VMEM((2, 4, 128, 128), BF16),
            pltpu.VMEM((8, 128), F32),
            pltpu.VMEM((1024, 128), F32),
            pltpu.VMEM((2, 128, 16, 128), BF16),
            pltpu.VMEM((2, 128, 16, 128), BF16),
            pltpu.VMEM((4, 256, 128), BF16),
            pltpu.VMEM((2, 4, 256, 128), BF16),
            pltpu.VMEM((2, 512, 128), BF16),
            pltpu.VMEM((2, 2, 512, 128), BF16),
            pltpu.VMEM((2, 64, 16, 128), BF16),
            pltpu.VMEM((2, 64, 16, 128), BF16),
            pltpu.VMEM((2, 8, 64, 128), BF16),
            pltpu.VMEM((2, 2, 8, 64, 128), BF16),
            pltpu.SemaphoreType.DMA((11,)),
            dma, pltpu.SemaphoreType.DMA((2, 4)), dma, dma, dma, dma, dma, dma,
            pltpu.SemaphoreType.REGULAR,
        ],
        compiler_params=pltpu.CompilerParams(
            collective_id=0, has_side_effects=True, vmem_limit_bytes=56 * 1024 * 1024
        ),
        name="triangles",
    )(
        pair_rep.reshape(4, 8, 32, 128),
        residue_mask.reshape(1, 512),
        input_weights,
        gate_weights,
        output_weights,
    )
    return out


def solution(mesh):
    placed = (P("row", "col", None), P(), P(), P(), P())
    return jax.shard_map(
        per_device, mesh=mesh, in_specs=placed, out_specs=P("row", "col", None), check_vma=False
    )
```

```python
import functools

import jax
import jax.numpy as jnp
from jax import lax
from jax.experimental import pallas as pl
from jax.experimental.pallas import tpu as pltpu
from jax.sharding import PartitionSpec as P

EPS = 1e-05
MESH = pl.DeviceIdType.MESH
F32 = jnp.float32
BF16 = jnp.bfloat16


def sigmoid(x):
    return 0.5 * jnp.tanh(0.5 * x) + 0.5


def swap_blocks(parts):
    group = lax.broadcasted_iota(jnp.int32, parts[0].shape, parts[0].ndim - 1) // 32
    axis = parts[0].ndim - 1
    high = group >= 2
    odd = lax.rem(group, 2) == 1

    def far(a, b):
        c = pltpu.roll(jnp.where(high, a, b), 64, axis)
        return jnp.where(high, c, a), jnp.where(high, b, c)

    def near(a, b):
        c = jnp.where(odd, a, b)
        return jnp.where(odd, pltpu.roll(c, 32, axis), a), jnp.where(odd, b, pltpu.roll(c, 96, axis))

    p0, p2 = far(parts[0], parts[2])
    p1, p3 = far(parts[1], parts[3])
    p0, p1 = near(p0, p1)
    p2, p3 = near(p2, p3)
    return p0, p1, p2, p3


def far_first(step):
    pair, second = step // 2, lax.rem(step, 2)
    middle = (pair == 1) | (pair == 2)
    dx = jnp.where(middle, 1 + 2 * second, jnp.where(pair == 0, 2, 0))
    return dx, jnp.where(middle, 2 - pair, 1 - second)


ALONG_Z = (4, 3, 5, 2, 6, 1, 7, 0)


def kernel(
    z_hbm, mask_ref, win_hbm, wgate_hbm, wout_hbm, out_ref,
    zp, win, wgate, wout, wfin, normed, wt, mask8, gate,
    send1, recv1, left0, right0, left1, right1, send2, recv2, stage, fin,
    load, sem1s, sem1r, semxs, semxr, sem2s, sem2r, semfs, semfr, ready,
):
    r, c = lax.axis_index("row"), lax.axis_index("col")
    cc, core = c // 2, lax.rem(c, 2)
    y, z = r // 8, lax.rem(r, 8)
    x, yh = cc // 2, lax.rem(cc, 2)
    me = cc * 16 + r
    sibling = (r, cc * 2 + 1 - core)

    barrier = pltpu.get_barrier_semaphore()

    for dz in ALONG_Z:
        row = core * 8 + lax.rem(z + dz, 8)
        for k in range(2):
            far = lax.rem(x + 2, 4) * 4 + (1 - yh) * 2 + k
            pl.semaphore_signal(barrier, inc=1, device_id=(row, far), device_id_type=MESH)

    @pl.loop(1, 8)
    def _(t):
        peer = lax.rem(cc + t, 8) * 2 + core
        pl.semaphore_signal(barrier, inc=1, device_id=(r, peer), device_id_type=MESH)

    loads = [pltpu.make_async_copy(z_hbm.at[:, t], zp.at[t], load.at[t]) for t in range(8)]
    loads.append(pltpu.make_async_copy(win_hbm, win, load.at[8]))
    loads.append(pltpu.make_async_copy(wgate_hbm, wgate, load.at[9]))
    loads.append(pltpu.make_async_copy(wout_hbm, wout, load.at[10]))
    for one in loads:
        one.start()

    valid = jnp.broadcast_to(mask_ref[...].astype(F32), (8, 512))
    n8 = lax.broadcasted_iota(jnp.int32, (8, 512), 1)
    t8 = lax.broadcasted_iota(jnp.int32, (8, 512), 0)
    n = lax.broadcasted_iota(jnp.int32, (512, 128), 0)
    l = lax.broadcasted_iota(jnp.int32, (512, 128), 1)
    rows = jnp.where(lax.rem(n8, 8) == t8, valid, 0.0).astype(BF16)
    pick_row = jnp.where(n // 8 == 4 * r + l // 32, 1.0, 0.0).astype(BF16)
    pick_col = jnp.where(n == 32 * c + lax.rem(l, 32), 1.0, 0.0).astype(BF16)
    mask8[...] = jnp.dot(rows, pick_row, preferred_element_type=F32) * jnp.dot(
        valid.astype(BF16), pick_col, preferred_element_type=F32
    )

    def normalize_rows(t, v):
        centred = v - jnp.mean(v, axis=-1, keepdims=True)
        variance = jnp.mean(centred * centred, axis=-1, keepdims=True)
        normed[pl.ds(t * 128, 128), :] = (centred * lax.rsqrt(variance + EPS)).astype(BF16)

    def turn_weights(u):
        for k in range(4):
            wt[u, k] = win[u, :, k * 128 : (k + 1) * 128].astype(F32).T.astype(BF16)

    def project(step, update):
        dx, dh = far_first(step)
        chip = lax.rem(x + dx, 4) * 2 + lax.rem(yh + dh, 2)
        at = pl.ds(pl.multiple_of(chip * 16, 16), 16)
        w = jnp.concatenate([wt[update, k, at, :] for k in range(4)], axis=0)
        p = lax.dot_general(w, normed[...], (((1,), (1,)), ((), ())), preferred_element_type=F32)
        both = []
        for k in (0, 32):
            side = sigmoid(p[k + 16 : k + 32]) * p[k : k + 16]
            tiles = jnp.stack([side[:, t * 128 : (t + 1) * 128] for t in range(8)], axis=0)
            both.append(jnp.swapaxes(tiles, 0, 1) * mask8[...][None])
        send1[update, at] = jnp.concatenate(both, axis=1).astype(BF16)

    for t in range(8):
        loads[t].wait()
        normalize_rows(t, zp[t].reshape(128, 128).astype(F32))
    loads[8].wait()
    turn_weights(0)

    for update in range(2):
        half = y if update == 0 else c // 8
        corner = lax.rem(c, 4)
        slot = x * 32 + z * 4 + corner if update == 0 else lax.rem(x, 2) * 64 + r * 4 + corner
        own = half == core

        def spread(step, carry, update=update, half=half, own=own, slot=slot):
            if update == 1:
                project(step, 1)
            dx, dh = far_first(step)
            chip = lax.rem(x + dx, 4) * 2 + lax.rem(yh + dh, 2)

            def send(row):
                pltpu.make_async_remote_copy(
                    src_ref=send1.at[update, chip * 16 + row],
                    dst_ref=recv1.at[update, slot],
                    send_sem=sem1s.at[update],
                    recv_sem=sem1r.at[update, dx],
                    device_id=(row, chip * 2 + half),
                    device_id_type=MESH,
                ).start()

            far, near = lax.rem(y + 1 - dh, 2) * 8, lax.rem(y + dh, 2) * 8
            for line in (far, near):
                for dz in ALONG_Z[:-1]:
                    send(line + lax.rem(z + dz, 8))
                if line is far:
                    send(line + z)
            here = (step == 7) & own

            @pl.when(jnp.logical_not(here))
            def _():
                send(near + z)

            @pl.when(here)
            def _():
                pltpu.make_async_copy(send1.at[update, me], recv1.at[update, slot], sem1r.at[update, dx]).start()

            return carry

        if update == 0:
            project(0, 0)
            pl.semaphore_wait(barrier, 23)

            @pl.loop(1, 8)
            def _(t):
                peer = lax.rem(cc + t, 8) * 2 + core
                pl.semaphore_signal(ready, inc=1, device_id=(r, peer), device_id_type=MESH)

            spread(0, 0)

            @pl.loop(1, 8)
            def _(step):
                project(step, 0)

            pl.semaphore_wait(ready, 7)
            lax.fori_loop(1, 8, spread, 0)
        else:
            lax.fori_loop(0, 8, spread, 0)

        if update == 0:
            turn_weights(1)
            loads[9].wait()
            loads[10].wait()
            for u in range(2):
                w = wout[u].astype(F32).reshape(8, 2, 8, 128)
                wfin[u] = jnp.concatenate([w[:, k].reshape(64, 128) for k in range(2)], axis=0).astype(BF16)

        @pl.loop(0, 4)
        def _(i, update=update):
            at = pl.ds(pl.multiple_of(i * 256, 256), 256)
            gate[at, :] = sigmoid(jnp.dot(normed[at, :], wgate[update], preferred_element_type=F32))

        left, right = (left0, right0) if update == 0 else (left1, right1)
        columns = 4 if update == 0 else 2
        count = 128 // columns

        def arrive(dx, update=update, left=left, right=right, columns=columns, count=count):
            k = lax.rem(x + 4 - dx, columns)
            got = recv1.at[update, pl.ds(0, count)]
            pltpu.make_async_copy(got, got, sem1r.at[update, dx]).wait()
            for part in range(count // 32):
                at = pl.ds(part * 256, 256)
                v = recv1[update, pl.ds(k * count + part * 32, 32)].astype(F32).reshape(8, 4, 16, 128)
                parts = swap_blocks([v[:, q] for q in range(4)])
                for side in range(2):
                    rows = jnp.stack([p[:, side * 8 : side * 8 + 8] for p in parts], axis=1)
                    rows = rows.reshape(256, 128).astype(BF16)
                    if side == 0:
                        left[k, at, :] = rows
                    else:
                        right[core, k, at, :] = rows
            part = right.at[core, k]
            pltpu.make_async_remote_copy(
                src_ref=part, dst_ref=part, send_sem=semxs.at[update], recv_sem=semxr.at[update],
                device_id=sibling, device_id_type=MESH,
            ).start()

        if update == 0:

            def each(i, carry, arrive=arrive):
                arrive(jnp.where(i == 0, 2, jnp.where(i == 3, 0, 2 * i - 1)))
                return carry

            lax.fori_loop(0, 4, each, 0)
        else:
            ways = lax.rem(x + 4 - core * 2, 4)
            other = lax.rem(ways + 3, 4)
            even, odd = jnp.where(lax.rem(ways, 2) == 0, ways, other), jnp.where(lax.rem(ways, 2) == 0, other, ways)
            arrive(jnp.where(even == 2, even, odd))
            arrive(jnp.where(even == 2, odd, even))
        origin = cc * 8 + z
        own_back = y == core
        way = lax.rem(core * 2 + 4 - x, 4)
        own_far = (way == 2) | (way == 1)
        own_odd = jnp.where(lax.rem(way, 2) == 1, way, lax.rem(way + 1, 4))

        def back(i, carry, update=update, left=left, right=right):
            first = jnp.where(own_far, 2, own_odd)
            second = jnp.where(own_far, own_odd, 2)
            dx = jnp.where(i == 0, first, jnp.where(i == 1, second, jnp.where(i == 2, 4 - own_odd, 0)))
            k = lax.rem(x + dx, 4)
            if update == 0:
                some = pl.ds(pl.multiple_of(lax.rem(k, 2) * 128, 128), 128)
                lhs = jnp.concatenate([left[q] for q in range(4)], axis=1)
                rhs = jnp.concatenate([right[k // 2, q, some, :] for q in range(4)], axis=1)
                v = lax.dot_general(lhs, rhs, (((1,), (1,)), ((), ())), preferred_element_type=F32)
            else:
                lhs = jnp.concatenate([left[q] for q in range(2)], axis=1)
                rhs = right[k // 2, lax.rem(k, 2)]
                v = lax.dot_general(lhs, rhs, (((0,), (0,)), ((), ())), preferred_element_type=F32)
            v = v.reshape(8, 4, 8, 128)
            parts = swap_blocks([v[:, u] for u in range(4)])
            for h in range(2):
                pair = jnp.concatenate([parts[2 * h], parts[2 * h + 1]], axis=1).astype(BF16)
                send2[update, pl.ds((k * 2 + h) * 8, 8)] = pair

            def send(chip, b):
                pltpu.make_async_remote_copy(
                    src_ref=send2.at[update, chip * 8 + b],
                    dst_ref=recv2.at[update, origin],
                    send_sem=sem2s.at[update],
                    recv_sem=sem2r.at[update],
                    device_id=(core * 8 + b, chip * 2 + y),
                    device_id_type=MESH,
                ).start()

            far, near = k * 2 + 1 - yh, k * 2 + yh
            for chip in (far, near):
                for dz in ALONG_Z[:-1]:
                    send(chip, lax.rem(z + dz, 8))
                if chip is far:
                    send(chip, z)
            here = (i == 3) & own_back

            @pl.when(jnp.logical_not(here))
            def _():
                send(near, z)

            @pl.when(here)
            def _():
                pltpu.make_async_copy(
                    send2.at[update, cc * 8 + z], recv2.at[update, origin], sem2r.at[update]
                ).start()

            return carry

        back(0, 0)
        theirs = right.at[1 - core]
        pltpu.make_async_copy(theirs, theirs, semxr.at[update]).wait()
        lax.fori_loop(1, 4, back, 0)
        pltpu.make_async_copy(recv2.at[update], recv2.at[update], sem2r.at[update]).wait()

        v = jnp.swapaxes(recv2[update].astype(F32), 0, 1)
        first, second = v[0:8], v[8:16]
        low = core == 0
        stage[update] = jnp.where(low, second, first).astype(BF16)
        cross = pltpu.make_async_remote_copy(
            src_ref=stage.at[update], dst_ref=fin.at[update, core],
            send_sem=semfs.at[update], recv_sem=semfr.at[update],
            device_id=sibling, device_id_type=MESH,
        )
        cross.start()
        fin[update, core] = jnp.where(low, first, second).astype(BF16)
        other = fin.at[update, 1 - core]
        pltpu.make_async_copy(other, other, semfr.at[update]).wait()

        def finish(t, carry, update=update):
            v = jnp.concatenate([fin[update, 0, t], fin[update, 1, t]], axis=0).astype(F32)
            centred = v - jnp.mean(v, axis=0, keepdims=True)
            variance = jnp.mean(centred * centred, axis=0, keepdims=True)
            v = (centred * lax.rsqrt(variance + EPS)).astype(BF16)
            term = lax.dot_general(v, wfin[update], (((0,), (0,)), ((), ())), preferred_element_type=F32)
            at = pl.ds(pl.multiple_of(t * 128, 128), 128)
            new = zp[t].reshape(128, 128).astype(F32) + gate[at, :] * term
            if update == 0:
                new = new.astype(BF16)
                zp[t] = new.reshape(4, 32, 128)
                normalize_rows(t, new.astype(F32))
            else:
                for u in range(4):
                    out_ref[u * 8 + t] = new[u * 32 : u * 32 + 32]
            return carry

        lax.fori_loop(0, 8, finish, 0, unroll=8)

        mine = right.at[core]
        pltpu.make_async_copy(mine, mine, semxs.at[update]).wait()
        cross.wait_send()
        for sent, sem, all_remote, count in (
            (send1, sem1s, jnp.logical_not(own), 128),
            (send2, sem2s, jnp.logical_not(own_back), 64),
        ):

            @pl.when(all_remote)
            def _(update=update, sent=sent, sem=sem):
                pltpu.make_async_copy(sent.at[update], sent.at[update], sem.at[update]).wait()

            @pl.when(jnp.logical_not(all_remote))
            def _(update=update, sent=sent, sem=sem, count=count):
                gone = sent.at[update, pl.ds(0, count - 1)]
                pltpu.make_async_copy(gone, gone, sem.at[update]).wait()


def per_device(pair_rep, residue_mask, input_weights, gate_weights, output_weights):
    vmem = pl.BlockSpec(memory_space=pltpu.VMEM)
    anywhere = pl.BlockSpec(memory_space=pl.ANY)
    dma = pltpu.SemaphoreType.DMA((2,))
    out = pl.pallas_call(
        kernel,
        out_shape=jax.ShapeDtypeStruct((32, 32, 128), F32),
        in_specs=[anywhere, vmem, anywhere, anywhere, anywhere],
        out_specs=vmem,
        scratch_shapes=[
            pltpu.VMEM((8, 4, 32, 128), BF16),
            pltpu.VMEM((2, 128, 512), BF16),
            pltpu.VMEM((2, 128, 128), BF16),
            pltpu.VMEM((2, 128, 128), BF16),
            pltpu.VMEM((2, 128, 128), BF16),
            pltpu.VMEM((1024, 128), BF16),
            pltpu.VMEM((2, 4, 128, 128), BF16),
            pltpu.VMEM((8, 128), F32),
            pltpu.VMEM((1024, 128), F32),
            pltpu.VMEM((2, 128, 16, 128), BF16),
            pltpu.VMEM((2, 128, 16, 128), BF16),
            pltpu.VMEM((4, 256, 128), BF16),
            pltpu.VMEM((2, 4, 256, 128), BF16),
            pltpu.VMEM((2, 512, 128), BF16),
            pltpu.VMEM((2, 2, 512, 128), BF16),
            pltpu.VMEM((2, 64, 16, 128), BF16),
            pltpu.VMEM((2, 64, 16, 128), BF16),
            pltpu.VMEM((2, 8, 64, 128), BF16),
            pltpu.VMEM((2, 2, 8, 64, 128), BF16),
            pltpu.SemaphoreType.DMA((11,)),
            dma, pltpu.SemaphoreType.DMA((2, 4)), dma, dma, dma, dma, dma, dma,
            pltpu.SemaphoreType.REGULAR,
        ],
        compiler_params=pltpu.CompilerParams(
            collective_id=0, has_side_effects=True, vmem_limit_bytes=56 * 1024 * 1024
        ),
        name="triangles",
    )(
        pair_rep.reshape(4, 8, 32, 128),
        residue_mask.reshape(1, 512),
        input_weights,
        gate_weights,
        output_weights,
    )
    return out.astype(BF16)


def solution(mesh):
    placed = (P("row", "col", None), P(), P(), P(), P())
    return jax.shard_map(
        per_device, mesh=mesh, in_specs=placed, out_specs=P("row", "col", None), check_vma=False
    )
```

```python
import functools

import jax
import jax.numpy as jnp
from jax import lax
from jax.experimental import pallas as pl
from jax.experimental.pallas import tpu as pltpu
from jax.sharding import PartitionSpec as P

EPS = 1e-05
MESH = pl.DeviceIdType.MESH
F32 = jnp.float32
BF16 = jnp.bfloat16


def sigmoid(x):
    return 0.5 * jnp.tanh(0.5 * x) + 0.5


def swap_blocks(parts):
    group = lax.broadcasted_iota(jnp.int32, parts[0].shape, parts[0].ndim - 1) // 32
    axis = parts[0].ndim - 1
    high = group >= 2
    odd = lax.rem(group, 2) == 1

    def far(a, b):
        c = pltpu.roll(jnp.where(high, a, b), 64, axis)
        return jnp.where(high, c, a), jnp.where(high, b, c)

    def near(a, b):
        c = jnp.where(odd, a, b)
        return jnp.where(odd, pltpu.roll(c, 32, axis), a), jnp.where(odd, b, pltpu.roll(c, 96, axis))

    p0, p2 = far(parts[0], parts[2])
    p1, p3 = far(parts[1], parts[3])
    p0, p1 = near(p0, p1)
    p2, p3 = near(p2, p3)
    return p0, p1, p2, p3


def far_first(step):
    pair, second = step // 2, lax.rem(step, 2)
    middle = (pair == 1) | (pair == 2)
    dx = jnp.where(middle, 1 + 2 * second, jnp.where(pair == 0, 2, 0))
    return dx, jnp.where(middle, 2 - pair, 1 - second)


ALONG_Z = ((4, 3), (2, 5), (6, 1), (0, 7))


def kernel(
    z_hbm, mask_hbm, win_hbm, wgate_hbm, wout_hbm, out_ref,
    zp, mask_ref, win, wgate, wout, wfin, normed, wt, mask8, gate,
    send1, recv1, left0, right0, left1, right1, send2, recv2, stage, fin,
    load, sem1s, sem1r, semxs, semxr, sem2s, sem2r, semfs, semfr, ready,
):
    r, c = lax.axis_index("row"), lax.axis_index("col")
    cc, core = c // 2, lax.rem(c, 2)
    y, z = r // 8, lax.rem(r, 8)
    x, yh = cc // 2, lax.rem(cc, 2)
    me = cc * 16 + r
    sibling = (r, cc * 2 + 1 - core)

    barrier = pltpu.get_barrier_semaphore()

    for dz in (4, 3, 5, 2, 6, 1, 7, 0):
        row = core * 8 + lax.rem(z + dz, 8)
        for k in range(2):
            far = lax.rem(x + 2, 4) * 4 + (1 - yh) * 2 + k
            pl.semaphore_signal(barrier, inc=1, device_id=(row, far), device_id_type=MESH)

    @pl.loop(1, 8)
    def _(t):
        peer = lax.rem(cc + t, 8) * 2 + core
        pl.semaphore_signal(barrier, inc=1, device_id=(r, peer), device_id_type=MESH)

    loads = [pltpu.make_async_copy(z_hbm.at[:, t], zp.at[t], load.at[t]) for t in range(8)]
    loads.append(pltpu.make_async_copy(win_hbm, win, load.at[8]))
    loads.append(pltpu.make_async_copy(wgate_hbm, wgate, load.at[9]))
    loads.append(pltpu.make_async_copy(wout_hbm, wout, load.at[10]))
    loads.append(pltpu.make_async_copy(mask_hbm, mask_ref, load.at[11]))
    for one in loads:
        one.start()

    loads[11].wait()
    valid = jnp.broadcast_to(mask_ref[...].astype(F32), (8, 512))
    n8 = lax.broadcasted_iota(jnp.int32, (8, 512), 1)
    t8 = lax.broadcasted_iota(jnp.int32, (8, 512), 0)
    n = lax.broadcasted_iota(jnp.int32, (512, 128), 0)
    l = lax.broadcasted_iota(jnp.int32, (512, 128), 1)
    rows = jnp.where(lax.rem(n8, 8) == t8, valid, 0.0).astype(BF16)
    pick_row = jnp.where(n // 8 == 4 * r + l // 32, 1.0, 0.0).astype(BF16)
    pick_col = jnp.where(n == 32 * c + lax.rem(l, 32), 1.0, 0.0).astype(BF16)
    mask8[...] = jnp.dot(rows, pick_row, preferred_element_type=F32) * jnp.dot(
        valid.astype(BF16), pick_col, preferred_element_type=F32
    )

    def normalize_rows(t, v):
        centred = v - jnp.mean(v, axis=-1, keepdims=True)
        variance = jnp.mean(centred * centred, axis=-1, keepdims=True)
        normed[pl.ds(t * 128, 128), :] = (centred * lax.rsqrt(variance + EPS)).astype(BF16)

    def turn_weights(u):
        for k in range(4):
            wt[u, k] = win[u, :, k * 128 : (k + 1) * 128].astype(F32).T.astype(BF16)

    def project(step, update):
        dx, dh = far_first(step)
        chip = lax.rem(x + dx, 4) * 2 + lax.rem(yh + dh, 2)
        at = pl.ds(pl.multiple_of(chip * 16, 16), 16)
        w = jnp.concatenate([wt[update, k, at, :] for k in range(4)], axis=0)
        p = lax.dot_general(w, normed[...], (((1,), (1,)), ((), ())), preferred_element_type=F32)
        both = []
        for k in (0, 32):
            side = sigmoid(p[k + 16 : k + 32]) * p[k : k + 16]
            tiles = jnp.stack([side[:, t * 128 : (t + 1) * 128] for t in range(8)], axis=0)
            both.append(jnp.swapaxes(tiles, 0, 1) * mask8[...][None])
        send1[update, at] = jnp.concatenate(both, axis=1).astype(BF16)

    for t in range(8):
        loads[t].wait()
        normalize_rows(t, zp[t].reshape(128, 128).astype(F32))
    loads[8].wait()
    turn_weights(0)

    for update in range(2):
        half = y if update == 0 else c // 8
        corner = lax.rem(c, 4)
        slot = x * 32 + z * 4 + corner if update == 0 else lax.rem(x, 2) * 64 + r * 4 + corner
        own = half == core

        def spread(step, update=update, half=half, own=own, slot=slot):
            dx, dh = far_first(step)
            chip = lax.rem(x + dx, 4) * 2 + lax.rem(yh + dh, 2)

            def send(row):
                pltpu.make_async_remote_copy(
                    src_ref=send1.at[update, chip * 16 + row],
                    dst_ref=recv1.at[update, slot],
                    send_sem=sem1s.at[update],
                    recv_sem=sem1r.at[update, dx],
                    device_id=(row, chip * 2 + half),
                    device_id_type=MESH,
                ).start()

            near = lax.rem(y + dh, 2)
            for parity, line in ((0, 1 - near), (0, near), (1, 1 - near), (1, near)):
                odd = lax.rem(parity + line + z + chip // 2 + chip, 2) == 1
                for way, dz in enumerate(ALONG_Z):
                    row = line * 8 + lax.rem(z + jnp.where(odd, dz[1], dz[0]), 8)
                    if way < 3 or line is not near:
                        send(row)
                        continue
                    here = (step == 7) & own & jnp.logical_not(odd)

                    @pl.when(jnp.logical_not(here))
                    def _(row=row):
                        send(row)

                    @pl.when(here)
                    def _():
                        pltpu.make_async_copy(
                            send1.at[update, me], recv1.at[update, slot], sem1r.at[update, dx]
                        ).start()

        if update == 0:
            project(0, 0)
            pl.semaphore_wait(barrier, 23)

            def tell(step, carry):
                dx, dh = far_first(step)
                peer = lax.rem(x + 6 - dx, 4) * 4 + lax.rem(1 + yh + dh, 2) * 2 + core
                pl.semaphore_signal(ready.at[step], inc=1, device_id=(r, peer), device_id_type=MESH)
                return carry

            lax.fori_loop(1, 8, tell, 0)
            spread(0)

            @pl.loop(1, 8)
            def _(step):
                project(step, 0)

            @pl.loop(1, 8)
            def _(step, spread=spread):
                pl.semaphore_wait(ready.at[step], 1)
                spread(step)

        else:

            @pl.loop(0, 8)
            def _(step, spread=spread):
                project(step, 1)
                spread(step)

        if update == 0:
            turn_weights(1)
            loads[9].wait()
            loads[10].wait()
            for u in range(2):
                w = wout[u].astype(F32).reshape(8, 2, 8, 128)
                wfin[u] = jnp.concatenate([w[:, k].reshape(64, 128) for k in range(2)], axis=0).astype(BF16)

        @pl.loop(0, 4)
        def _(i, update=update):
            at = pl.ds(pl.multiple_of(i * 256, 256), 256)
            gate[at, :] = sigmoid(jnp.dot(normed[at, :], wgate[update], preferred_element_type=F32))

        left, right = (left0, right0) if update == 0 else (left1, right1)
        columns = 4 if update == 0 else 2
        count = 128 // columns

        def arrive(dx, update=update, left=left, right=right, columns=columns, count=count):
            k = lax.rem(x + 4 - dx, columns)
            got = recv1.at[update, pl.ds(0, count)]
            pltpu.make_async_copy(got, got, sem1r.at[update, dx]).wait()
            for part in range(count // 32):
                at = pl.ds(part * 256, 256)
                v = recv1[update, pl.ds(k * count + part * 32, 32)].astype(F32).reshape(8, 4, 16, 128)
                parts = swap_blocks([v[:, q] for q in range(4)])
                for side in range(2):
                    rows = jnp.stack([p[:, side * 8 : side * 8 + 8] for p in parts], axis=1)
                    rows = rows.reshape(256, 128).astype(BF16)
                    if side == 0:
                        left[k, at, :] = rows
                    else:
                        right[core, k, at, :] = rows
            part = right.at[core, k]
            pltpu.make_async_remote_copy(
                src_ref=part, dst_ref=part, send_sem=semxs.at[update], recv_sem=semxr.at[update],
                device_id=sibling, device_id_type=MESH,
            ).start()

        if update == 0:

            def each(i, carry, arrive=arrive):
                arrive(jnp.where(i == 0, 2, jnp.where(i == 3, 0, 2 * i - 1)))
                return carry

            lax.fori_loop(0, 4, each, 0)
        else:
            ways = lax.rem(x + 4 - core * 2, 4)
            other = lax.rem(ways + 3, 4)
            even, odd = jnp.where(lax.rem(ways, 2) == 0, ways, other), jnp.where(lax.rem(ways, 2) == 0, other, ways)
            arrive(jnp.where(even == 2, even, odd))
            arrive(jnp.where(even == 2, odd, even))
        origin = cc * 8 + z
        own_back = y == core
        way = lax.rem(core * 2 + 4 - x, 4)
        own_far = (way == 2) | (way == 1)
        own_odd = jnp.where(lax.rem(way, 2) == 1, way, lax.rem(way + 1, 4))

        def block_of(i, own_far=own_far, own_odd=own_odd):
            first = jnp.where(own_far, 2, own_odd)
            second = jnp.where(own_far, own_odd, 2)
            dx = jnp.where(i == 0, first, jnp.where(i == 1, second, jnp.where(i == 2, 4 - own_odd, 0)))
            return lax.rem(x + dx, 4)

        def back_sends(i, update=update, block_of=block_of, origin=origin, own_back=own_back):
            k = block_of(i)

            def send(chip, b):
                pltpu.make_async_remote_copy(
                    src_ref=send2.at[update, chip * 8 + b],
                    dst_ref=recv2.at[update, origin],
                    send_sem=sem2s.at[update],
                    recv_sem=sem2r.at[update],
                    device_id=(core * 8 + b, chip * 2 + y),
                    device_id_type=MESH,
                ).start()

            for parity, h in ((0, 1 - yh), (0, yh), (1, 1 - yh), (1, yh)):
                odd = lax.rem(parity + core + z + k + h, 2) == 1
                for way, dz in enumerate(ALONG_Z):
                    b = lax.rem(z + jnp.where(odd, dz[1], dz[0]), 8)
                    if way < 3 or h is not yh:
                        send(k * 2 + h, b)
                        continue
                    here = (i == 3) & own_back & jnp.logical_not(odd)

                    @pl.when(jnp.logical_not(here))
                    def _(h=h, b=b):
                        send(k * 2 + h, b)

                    @pl.when(here)
                    def _():
                        pltpu.make_async_copy(
                            send2.at[update, cc * 8 + z], recv2.at[update, origin], sem2r.at[update]
                        ).start()

        def back(i, carry, update=update, left=left, right=right, block_of=block_of, back_sends=back_sends):
            k = block_of(i)
            if update == 0:
                some = pl.ds(pl.multiple_of(lax.rem(k, 2) * 128, 128), 128)
                lhs = jnp.concatenate([left[q] for q in range(4)], axis=1)
                rhs = jnp.concatenate([right[k // 2, q, some, :] for q in range(4)], axis=1)
                v = lax.dot_general(lhs, rhs, (((1,), (1,)), ((), ())), preferred_element_type=F32)
            else:
                lhs = jnp.concatenate([left[q] for q in range(2)], axis=1)
                rhs = right[k // 2, lax.rem(k, 2)]
                v = lax.dot_general(lhs, rhs, (((0,), (0,)), ((), ())), preferred_element_type=F32)
            v = v.reshape(8, 4, 8, 128)
            parts = swap_blocks([v[:, u] for u in range(4)])
            for h in range(2):
                pair = jnp.concatenate([parts[2 * h], parts[2 * h + 1]], axis=1).astype(BF16)
                send2[update, pl.ds((k * 2 + h) * 8, 8)] = pair

            back_sends(i)
            return carry

        back(0, 0)
        theirs = right.at[1 - core]
        pltpu.make_async_copy(theirs, theirs, semxr.at[update]).wait()
        lax.fori_loop(1, 4, back, 0)
        pltpu.make_async_copy(recv2.at[update], recv2.at[update], sem2r.at[update]).wait()

        v = jnp.swapaxes(recv2[update].astype(F32), 0, 1)
        first, second = v[0:8], v[8:16]
        low = core == 0
        stage[update] = jnp.where(low, second, first).astype(BF16)
        cross = pltpu.make_async_remote_copy(
            src_ref=stage.at[update], dst_ref=fin.at[update, core],
            send_sem=semfs.at[update], recv_sem=semfr.at[update],
            device_id=sibling, device_id_type=MESH,
        )
        cross.start()
        fin[update, core] = jnp.where(low, first, second).astype(BF16)
        other = fin.at[update, 1 - core]
        pltpu.make_async_copy(other, other, semfr.at[update]).wait()

        def finish(t, carry, update=update):
            v = jnp.concatenate([fin[update, 0, t], fin[update, 1, t]], axis=0).astype(F32)
            centred = v - jnp.mean(v, axis=0, keepdims=True)
            variance = jnp.mean(centred * centred, axis=0, keepdims=True)
            v = (centred * lax.rsqrt(variance + EPS)).astype(BF16)
            term = lax.dot_general(v, wfin[update], (((0,), (0,)), ((), ())), preferred_element_type=F32)
            at = pl.ds(pl.multiple_of(t * 128, 128), 128)
            new = zp[t].reshape(128, 128).astype(F32) + gate[at, :] * term
            if update == 0:
                new = new.astype(BF16)
                zp[t] = new.reshape(4, 32, 128)
                normalize_rows(t, new.astype(F32))
            else:
                for u in range(4):
                    out_ref[u * 8 + t] = new[u * 32 : u * 32 + 32].astype(BF16)
            return carry

        lax.fori_loop(0, 8, finish, 0, unroll=8)

        mine = right.at[core]
        pltpu.make_async_copy(mine, mine, semxs.at[update]).wait()
        cross.wait_send()
        for sent, sem, all_remote, count in (
            (send1, sem1s, jnp.logical_not(own), 128),
            (send2, sem2s, jnp.logical_not(own_back), 64),
        ):

            @pl.when(all_remote)
            def _(update=update, sent=sent, sem=sem):
                pltpu.make_async_copy(sent.at[update], sent.at[update], sem.at[update]).wait()

            @pl.when(jnp.logical_not(all_remote))
            def _(update=update, sent=sent, sem=sem, count=count):
                gone = sent.at[update, pl.ds(0, count - 1)]
                pltpu.make_async_copy(gone, gone, sem.at[update]).wait()


def per_device(pair_rep, residue_mask, input_weights, gate_weights, output_weights):
    vmem = pl.BlockSpec(memory_space=pltpu.VMEM)
    anywhere = pl.BlockSpec(memory_space=pl.ANY)
    dma = pltpu.SemaphoreType.DMA((2,))
    out = pl.pallas_call(
        kernel,
        out_shape=jax.ShapeDtypeStruct((32, 32, 128), BF16),
        in_specs=[anywhere] * 5,
        out_specs=vmem,
        scratch_shapes=[
            pltpu.VMEM((8, 4, 32, 128), BF16),
            pltpu.VMEM((1, 512), jnp.int32),
            pltpu.VMEM((2, 128, 512), BF16),
            pltpu.VMEM((2, 128, 128), BF16),
            pltpu.VMEM((2, 128, 128), BF16),
            pltpu.VMEM((2, 128, 128), BF16),
            pltpu.VMEM((1024, 128), BF16),
            pltpu.VMEM((2, 4, 128, 128), BF16),
            pltpu.VMEM((8, 128), F32),
            pltpu.VMEM((1024, 128), F32),
            pltpu.VMEM((2, 128, 16, 128), BF16),
            pltpu.VMEM((2, 128, 16, 128), BF16),
            pltpu.VMEM((4, 256, 128), BF16),
            pltpu.VMEM((2, 4, 256, 128), BF16),
            pltpu.VMEM((2, 512, 128), BF16),
            pltpu.VMEM((2, 2, 512, 128), BF16),
            pltpu.VMEM((2, 64, 16, 128), BF16),
            pltpu.VMEM((2, 64, 16, 128), BF16),
            pltpu.VMEM((2, 8, 64, 128), BF16),
            pltpu.VMEM((2, 2, 8, 64, 128), BF16),
            pltpu.SemaphoreType.DMA((12,)),
            dma, pltpu.SemaphoreType.DMA((2, 4)), dma, dma, dma, dma, dma, dma,
            pltpu.SemaphoreType.REGULAR((8,)),
        ],
        compiler_params=pltpu.CompilerParams(
            collective_id=0, has_side_effects=True, vmem_limit_bytes=32 * 1024 * 1024
        ),
        name="triangles",
    )(
        pltpu.with_memory_space_constraint(pair_rep.reshape(4, 8, 32, 128), pltpu.HBM),
        pltpu.with_memory_space_constraint(residue_mask.reshape(1, 512), pltpu.HBM),
        pltpu.with_memory_space_constraint(input_weights, pltpu.HBM),
        pltpu.with_memory_space_constraint(gate_weights, pltpu.HBM),
        pltpu.with_memory_space_constraint(output_weights, pltpu.HBM),
    )
    return out


def solution(mesh):
    placed = (P("row", "col", None), P(), P(), P(), P())
    return jax.shard_map(
        per_device, mesh=mesh, in_specs=placed, out_specs=P("row", "col", None), check_vma=False
    )
```

```python
import functools

import jax
import jax.numpy as jnp
from jax import lax
from jax.experimental import pallas as pl
from jax.experimental.pallas import tpu as pltpu
from jax.sharding import PartitionSpec as P

EPS = 1e-05
MESH = pl.DeviceIdType.MESH
F32 = jnp.float32
BF16 = jnp.bfloat16


def sigmoid(x):
    return 0.5 * jnp.tanh(0.5 * x) + 0.5


def swap_blocks(parts):
    group = lax.broadcasted_iota(jnp.int32, parts[0].shape, parts[0].ndim - 1) // 32
    axis = parts[0].ndim - 1
    high = group >= 2
    odd = lax.rem(group, 2) == 1

    def far(a, b):
        c = pltpu.roll(jnp.where(high, a, b), 64, axis)
        return jnp.where(high, c, a), jnp.where(high, b, c)

    def near(a, b):
        c = jnp.where(odd, a, b)
        return jnp.where(odd, pltpu.roll(c, 32, axis), a), jnp.where(odd, b, pltpu.roll(c, 96, axis))

    p0, p2 = far(parts[0], parts[2])
    p1, p3 = far(parts[1], parts[3])
    p0, p1 = near(p0, p1)
    p2, p3 = near(p2, p3)
    return p0, p1, p2, p3


def far_first(step):
    pair, second = step // 2, lax.rem(step, 2)
    middle = (pair == 1) | (pair == 2)
    dx = jnp.where(middle, 1 + 2 * second, jnp.where(pair == 0, 2, 0))
    return dx, jnp.where(middle, 2 - pair, 1 - second)


ALONG_Z = ((4, 3), (2, 5), (6, 1), (0, 7))


def kernel(
    z_hbm, mask_hbm, win_hbm, wgate_hbm, wout_hbm, out_ref,
    zp, mask_ref, win, wgate, wout, normed, wt, mask8, gate,
    send1, recv1, left0, right0, left1, right1, send2, recv2,
    load, sem1s, sem1r, semxs, semxr, sem2s, sem2r, ready,
):
    r, c = lax.axis_index("row"), lax.axis_index("col")
    cc, core = c // 2, lax.rem(c, 2)
    y, z = r // 8, lax.rem(r, 8)
    x, yh = cc // 2, lax.rem(cc, 2)
    me = cc * 16 + r
    sibling = (r, cc * 2 + 1 - core)

    barrier = pltpu.get_barrier_semaphore()

    for dz in (4, 3, 5, 2, 6, 1, 7, 0):
        row = core * 8 + lax.rem(z + dz, 8)
        for k in range(2):
            far = lax.rem(x + 2, 4) * 4 + (1 - yh) * 2 + k
            pl.semaphore_signal(barrier, inc=1, device_id=(row, far), device_id_type=MESH)

    @pl.loop(1, 8)
    def _(t):
        peer = lax.rem(cc + t, 8) * 2 + core
        pl.semaphore_signal(barrier, inc=1, device_id=(r, peer), device_id_type=MESH)

    loads = [pltpu.make_async_copy(z_hbm.at[:, t], zp.at[t], load.at[t]) for t in range(8)]
    loads.append(pltpu.make_async_copy(win_hbm, win, load.at[8]))
    loads.append(pltpu.make_async_copy(wgate_hbm, wgate, load.at[9]))
    loads.append(pltpu.make_async_copy(wout_hbm, wout, load.at[10]))
    loads.append(pltpu.make_async_copy(mask_hbm, mask_ref, load.at[11]))
    for one in loads:
        one.start()

    loads[11].wait()
    valid = jnp.broadcast_to(mask_ref[...].astype(F32), (8, 512))
    n8 = lax.broadcasted_iota(jnp.int32, (8, 512), 1)
    t8 = lax.broadcasted_iota(jnp.int32, (8, 512), 0)
    n = lax.broadcasted_iota(jnp.int32, (512, 128), 0)
    l = lax.broadcasted_iota(jnp.int32, (512, 128), 1)
    rows = jnp.where(lax.rem(n8, 8) == t8, valid, 0.0).astype(BF16)
    pick_row = jnp.where(n // 8 == 4 * r + l // 32, 1.0, 0.0).astype(BF16)
    pick_col = jnp.where(n == 32 * c + lax.rem(l, 32), 1.0, 0.0).astype(BF16)
    mask8[...] = jnp.dot(rows, pick_row, preferred_element_type=F32) * jnp.dot(
        valid.astype(BF16), pick_col, preferred_element_type=F32
    )

    def normalize_rows(t, v):
        centred = v - jnp.mean(v, axis=-1, keepdims=True)
        variance = jnp.mean(centred * centred, axis=-1, keepdims=True)
        normed[pl.ds(t * 128, 128), :] = (centred * lax.rsqrt(variance + EPS)).astype(BF16)

    def turn_weights(u):
        for k in range(4):
            wt[u, k] = win[u, :, k * 128 : (k + 1) * 128].astype(F32).T.astype(BF16)

    def project(step, update):
        dx, dh = far_first(step)
        chip = lax.rem(x + dx, 4) * 2 + lax.rem(yh + dh, 2)
        at = pl.ds(pl.multiple_of(chip * 16, 16), 16)
        w = jnp.concatenate([wt[update, k, at, :] for k in range(4)], axis=0)
        p = lax.dot_general(w, normed[...], (((1,), (1,)), ((), ())), preferred_element_type=F32)
        both = []
        for k in (0, 32):
            side = sigmoid(p[k + 16 : k + 32]) * p[k : k + 16]
            tiles = jnp.stack([side[:, t * 128 : (t + 1) * 128] for t in range(8)], axis=0)
            both.append(jnp.swapaxes(tiles, 0, 1) * mask8[...][None])
        send1[update, at] = jnp.concatenate(both, axis=1).astype(BF16)

    for t in range(8):
        loads[t].wait()
        normalize_rows(t, zp[t].reshape(128, 128).astype(F32))
    loads[8].wait()
    turn_weights(0)

    for update in range(2):
        half = y if update == 0 else c // 8
        corner = lax.rem(c, 4)
        slot = x * 32 + z * 4 + corner if update == 0 else lax.rem(x, 2) * 64 + r * 4 + corner
        own = half == core

        def spread(step, update=update, half=half, own=own, slot=slot):
            dx, dh = far_first(step)
            chip = lax.rem(x + dx, 4) * 2 + lax.rem(yh + dh, 2)

            def send(row):
                pltpu.make_async_remote_copy(
                    src_ref=send1.at[update, chip * 16 + row],
                    dst_ref=recv1.at[update, slot],
                    send_sem=sem1s.at[update],
                    recv_sem=sem1r.at[update, dx],
                    device_id=(row, chip * 2 + half),
                    device_id_type=MESH,
                ).start()

            near = lax.rem(y + dh, 2)
            for parity, line in ((0, 1 - near), (0, near), (1, 1 - near), (1, near)):
                odd = lax.rem(parity + line + z + chip // 2 + chip, 2) == 1
                for way, dz in enumerate(ALONG_Z):
                    row = line * 8 + lax.rem(z + jnp.where(odd, dz[1], dz[0]), 8)
                    if way < 3 or line is not near:
                        send(row)
                        continue
                    here = (step == 7) & own & jnp.logical_not(odd)

                    @pl.when(jnp.logical_not(here))
                    def _(row=row):
                        send(row)

                    @pl.when(here)
                    def _():
                        pltpu.make_async_copy(
                            send1.at[update, me], recv1.at[update, slot], sem1r.at[update, dx]
                        ).start()

        if update == 0:
            project(0, 0)
            pl.semaphore_wait(barrier, 23)

            def tell(step, carry):
                dx, dh = far_first(step)
                peer = lax.rem(x + 6 - dx, 4) * 4 + lax.rem(1 + yh + dh, 2) * 2 + core
                pl.semaphore_signal(ready.at[step], inc=1, device_id=(r, peer), device_id_type=MESH)
                return carry

            lax.fori_loop(1, 8, tell, 0)
            spread(0)

            @pl.loop(1, 8)
            def _(step):
                project(step, 0)

            @pl.loop(1, 8)
            def _(step, spread=spread):
                pl.semaphore_wait(ready.at[step], 1)
                spread(step)

        else:

            @pl.loop(0, 8)
            def _(step, spread=spread):
                project(step, 1)
                spread(step)

        if update == 0:
            turn_weights(1)
            loads[9].wait()
            loads[10].wait()

        @pl.loop(0, 4)
        def _(i, update=update):
            at = pl.ds(pl.multiple_of(i * 256, 256), 256)
            gate[at, :] = sigmoid(jnp.dot(normed[at, :], wgate[update], preferred_element_type=F32))

        left, right = (left0, right0) if update == 0 else (left1, right1)
        columns = 4 if update == 0 else 2
        count = 128 // columns

        def arrive(dx, update=update, left=left, right=right, columns=columns, count=count):
            k = lax.rem(x + 4 - dx, columns)
            got = recv1.at[update, pl.ds(0, count)]
            pltpu.make_async_copy(got, got, sem1r.at[update, dx]).wait()
            for part in range(count // 32):
                at = pl.ds(part * 256, 256)
                v = recv1[update, pl.ds(k * count + part * 32, 32)].astype(F32).reshape(8, 4, 16, 128)
                parts = swap_blocks([v[:, q] for q in range(4)])
                for side in range(2):
                    rows = jnp.stack([p[:, side * 8 : side * 8 + 8] for p in parts], axis=1)
                    rows = rows.reshape(256, 128).astype(BF16)
                    if side == 0:
                        left[k, at, :] = rows
                    else:
                        right[core, k, at, :] = rows
            part = right.at[core, k]
            pltpu.make_async_remote_copy(
                src_ref=part, dst_ref=part, send_sem=semxs.at[update], recv_sem=semxr.at[update],
                device_id=sibling, device_id_type=MESH,
            ).start()

        if update == 0:

            def each(i, carry, arrive=arrive):
                arrive(jnp.where(i == 0, 2, jnp.where(i == 3, 0, 2 * i - 1)))
                return carry

            lax.fori_loop(0, 4, each, 0)
        else:
            ways = lax.rem(x + 4 - core * 2, 4)
            other = lax.rem(ways + 3, 4)
            even, odd = jnp.where(lax.rem(ways, 2) == 0, ways, other), jnp.where(lax.rem(ways, 2) == 0, other, ways)
            arrive(jnp.where(even == 2, even, odd))
            arrive(jnp.where(even == 2, odd, even))
        own_back = y == core
        way = lax.rem(core * 2 + 4 - x, 4)
        own_far = (way == 2) | (way == 1)
        own_odd = jnp.where(lax.rem(way, 2) == 1, way, lax.rem(way + 1, 4))

        def block_of(i, own_far=own_far, own_odd=own_odd):
            first = jnp.where(own_far, 2, own_odd)
            second = jnp.where(own_far, own_odd, 2)
            dx = jnp.where(i == 0, first, jnp.where(i == 1, second, jnp.where(i == 2, 4 - own_odd, 0)))
            return lax.rem(x + dx, 4)

        def back_sends(i, update=update, block_of=block_of, own_back=own_back):
            k = block_of(i)

            def send(col, b):
                pltpu.make_async_remote_copy(
                    src_ref=send2.at[update, col * 8 + b],
                    dst_ref=recv2.at[update, me],
                    send_sem=sem2s.at[update],
                    recv_sem=sem2r.at[update],
                    device_id=(core * 8 + b, col),
                    device_id_type=MESH,
                ).start()

            for parity, h in ((0, 1 - yh), (0, yh), (1, 1 - yh), (1, yh)):
                odd = lax.rem(parity + core + z + k + h, 2) == 1
                for way, dz in enumerate(ALONG_Z):
                    b = lax.rem(z + jnp.where(odd, dz[1], dz[0]), 8)
                    send(k * 4 + h * 2 + 1 - core, b)
                    if way < 3 or h is not yh:
                        send(k * 4 + h * 2 + core, b)
                        continue
                    here = (i == 3) & own_back & jnp.logical_not(odd)

                    @pl.when(jnp.logical_not(here))
                    def _(h=h, b=b):
                        send(k * 4 + h * 2 + core, b)

                    @pl.when(here)
                    def _():
                        pltpu.make_async_copy(
                            send2.at[update, c * 8 + z], recv2.at[update, me], sem2r.at[update]
                        ).start()

        def back(i, carry, update=update, left=left, right=right, block_of=block_of, back_sends=back_sends):
            k = block_of(i)
            if update == 0:
                some = pl.ds(pl.multiple_of(lax.rem(k, 2) * 128, 128), 128)
                lhs = jnp.concatenate([left[q] for q in range(4)], axis=1)
                rhs = jnp.concatenate([right[k // 2, q, some, :] for q in range(4)], axis=1)
                v = lax.dot_general(lhs, rhs, (((1,), (1,)), ((), ())), preferred_element_type=F32)
            else:
                lhs = jnp.concatenate([left[q] for q in range(2)], axis=1)
                rhs = right[k // 2, lax.rem(k, 2)]
                v = lax.dot_general(lhs, rhs, (((0,), (0,)), ((), ())), preferred_element_type=F32)
            v = v.reshape(8, 4, 8, 128)
            parts = swap_blocks([v[:, u] for u in range(4)])
            for q in range(4):
                send2[update, pl.ds((k * 4 + q) * 8, 8)] = parts[q].astype(BF16)

            back_sends(i)
            return carry

        back(0, 0)
        theirs = right.at[1 - core]
        pltpu.make_async_copy(theirs, theirs, semxr.at[update]).wait()
        lax.fori_loop(1, 4, back, 0)
        pltpu.make_async_copy(recv2.at[update], recv2.at[update], sem2r.at[update]).wait()

        tiles = jnp.swapaxes(recv2[update].astype(F32), 0, 1)
        for t in range(8):
            v = tiles[t]
            centred = v - jnp.mean(v, axis=0, keepdims=True)
            variance = jnp.mean(centred * centred, axis=0, keepdims=True)
            v = (centred * lax.rsqrt(variance + EPS)).astype(BF16)
            term = lax.dot_general(v, wout[update], (((0,), (0,)), ((), ())), preferred_element_type=F32)
            at = pl.ds(t * 128, 128)
            new = zp[t].reshape(128, 128).astype(F32) + gate[at, :] * term
            if update == 0:
                new = new.astype(BF16)
                zp[t] = new.reshape(4, 32, 128)
                normalize_rows(t, new.astype(F32))
            else:
                for u in range(4):
                    out_ref[u * 8 + t] = new[u * 32 : u * 32 + 32].astype(BF16)

        mine = right.at[core]
        pltpu.make_async_copy(mine, mine, semxs.at[update]).wait()
        for sent, sem, all_remote, count in (
            (send1, sem1s, jnp.logical_not(own), 128),
            (send2, sem2s, jnp.logical_not(own_back), 128),
        ):

            @pl.when(all_remote)
            def _(update=update, sent=sent, sem=sem):
                pltpu.make_async_copy(sent.at[update], sent.at[update], sem.at[update]).wait()

            @pl.when(jnp.logical_not(all_remote))
            def _(update=update, sent=sent, sem=sem, count=count):
                gone = sent.at[update, pl.ds(0, count - 1)]
                pltpu.make_async_copy(gone, gone, sem.at[update]).wait()


def per_device(pair_rep, residue_mask, input_weights, gate_weights, output_weights):
    vmem = pl.BlockSpec(memory_space=pltpu.VMEM)
    anywhere = pl.BlockSpec(memory_space=pl.ANY)
    dma = pltpu.SemaphoreType.DMA((2,))
    out = pl.pallas_call(
        kernel,
        out_shape=jax.ShapeDtypeStruct((32, 32, 128), BF16),
        in_specs=[anywhere] * 5,
        out_specs=vmem,
        scratch_shapes=[
            pltpu.VMEM((8, 4, 32, 128), BF16),
            pltpu.VMEM((1, 512), jnp.int32),
            pltpu.VMEM((2, 128, 512), BF16),
            pltpu.VMEM((2, 128, 128), BF16),
            pltpu.VMEM((2, 128, 128), BF16),
            pltpu.VMEM((1024, 128), BF16),
            pltpu.VMEM((2, 4, 128, 128), BF16),
            pltpu.VMEM((8, 128), F32),
            pltpu.VMEM((1024, 128), F32),
            pltpu.VMEM((2, 128, 16, 128), BF16),
            pltpu.VMEM((2, 128, 16, 128), BF16),
            pltpu.VMEM((4, 256, 128), BF16),
            pltpu.VMEM((2, 4, 256, 128), BF16),
            pltpu.VMEM((2, 512, 128), BF16),
            pltpu.VMEM((2, 2, 512, 128), BF16),
            pltpu.VMEM((2, 128, 8, 128), BF16),
            pltpu.VMEM((2, 128, 8, 128), BF16),
            pltpu.SemaphoreType.DMA((12,)),
            dma, pltpu.SemaphoreType.DMA((2, 4)), dma, dma, dma, dma,
            pltpu.SemaphoreType.REGULAR((8,)),
        ],
        compiler_params=pltpu.CompilerParams(
            collective_id=0, has_side_effects=True, vmem_limit_bytes=32 * 1024 * 1024
        ),
        name="triangles",
    )(
        pltpu.with_memory_space_constraint(pair_rep.reshape(4, 8, 32, 128), pltpu.HBM),
        pltpu.with_memory_space_constraint(residue_mask.reshape(1, 512), pltpu.HBM),
        pltpu.with_memory_space_constraint(input_weights, pltpu.HBM),
        pltpu.with_memory_space_constraint(gate_weights, pltpu.HBM),
        pltpu.with_memory_space_constraint(output_weights, pltpu.HBM),
    )
    return out


def solution(mesh):
    placed = (P("row", "col", None), P(), P(), P(), P())
    return jax.shard_map(
        per_device, mesh=mesh, in_specs=placed, out_specs=P("row", "col", None), check_vma=False
    )
```

```python
import functools

import jax
import jax.numpy as jnp
from jax import lax
from jax.experimental import pallas as pl
from jax.experimental.pallas import tpu as pltpu
from jax.sharding import PartitionSpec as P

EPS = 1e-05
MESH = pl.DeviceIdType.MESH
F32 = jnp.float32
BF16 = jnp.bfloat16


def sigmoid(x):
    return 0.5 * jnp.tanh(0.5 * x) + 0.5


def swap_blocks(parts):
    group = lax.broadcasted_iota(jnp.int32, parts[0].shape, parts[0].ndim - 1) // 32
    axis = parts[0].ndim - 1
    high = group >= 2
    odd = lax.rem(group, 2) == 1

    def far(a, b):
        c = pltpu.roll(jnp.where(high, a, b), 64, axis)
        return jnp.where(high, c, a), jnp.where(high, b, c)

    def near(a, b):
        c = jnp.where(odd, a, b)
        return jnp.where(odd, pltpu.roll(c, 32, axis), a), jnp.where(odd, b, pltpu.roll(c, 96, axis))

    p0, p2 = far(parts[0], parts[2])
    p1, p3 = far(parts[1], parts[3])
    p0, p1 = near(p0, p1)
    p2, p3 = near(p2, p3)
    return p0, p1, p2, p3


def far_first(step):
    pair, second = step // 2, lax.rem(step, 2)
    middle = (pair == 1) | (pair == 2)
    dx = jnp.where(middle, 1 + 2 * second, jnp.where(pair == 0, 2, 0))
    return dx, jnp.where(middle, 2 - pair, 1 - second)


ALONG_Z = ((4, 3), (2, 5), (6, 1), (0, 7))


def kernel(
    z_hbm, mask_hbm, win_hbm, wgate_hbm, wout_hbm, out_ref,
    zp, mask_ref, win, wgate, wout, normed, wt, mask8, gate,
    send1, recv1, left0, right0, left1, right1, send2, recv2,
    load, sem1s, sem1r, semxs, semxr, sem2s, sem2r, ready,
):
    r, c = lax.axis_index("row"), lax.axis_index("col")
    cc, core = c // 2, lax.rem(c, 2)
    y, z = r // 8, lax.rem(r, 8)
    x, yh = cc // 2, lax.rem(cc, 2)
    me = cc * 16 + r
    sibling = (r, cc * 2 + 1 - core)

    loads = [pltpu.make_async_copy(z_hbm.at[:, t], zp.at[t], load.at[t]) for t in range(8)]
    loads.append(pltpu.make_async_copy(win_hbm, win, load.at[8]))
    loads.append(pltpu.make_async_copy(wgate_hbm, wgate, load.at[9]))
    loads.append(pltpu.make_async_copy(wout_hbm, wout, load.at[10]))
    loads.append(pltpu.make_async_copy(mask_hbm, mask_ref, load.at[11]))
    for one in loads:
        one.start()

    barrier = pltpu.get_barrier_semaphore()

    for dz in (4, 3, 5, 2, 6, 1, 7, 0):
        row = core * 8 + lax.rem(z + dz, 8)
        for k in range(2):
            far = lax.rem(x + 2, 4) * 4 + (1 - yh) * 2 + k
            pl.semaphore_signal(barrier, inc=1, device_id=(row, far), device_id_type=MESH)

    @pl.loop(1, 8)
    def _(t):
        peer = lax.rem(cc + t, 8) * 2 + core
        pl.semaphore_signal(barrier, inc=1, device_id=(r, peer), device_id_type=MESH)

    n8 = lax.broadcasted_iota(jnp.int32, (8, 512), 1)
    t8 = lax.broadcasted_iota(jnp.int32, (8, 512), 0)
    n = lax.broadcasted_iota(jnp.int32, (512, 128), 0)
    l = lax.broadcasted_iota(jnp.int32, (512, 128), 1)
    pick_row = jnp.where(n // 8 == 4 * r + l // 32, 1.0, 0.0).astype(BF16)
    pick_col = jnp.where(n == 32 * c + lax.rem(l, 32), 1.0, 0.0).astype(BF16)
    loads[11].wait()
    valid = jnp.broadcast_to(mask_ref[...].astype(F32), (8, 512))
    rows = jnp.where(lax.rem(n8, 8) == t8, valid, 0.0).astype(BF16)
    mask8[...] = jnp.dot(rows, pick_row, preferred_element_type=F32) * jnp.dot(
        valid.astype(BF16), pick_col, preferred_element_type=F32
    )

    def normalize_rows(t, v):
        centred = v - jnp.mean(v, axis=-1, keepdims=True)
        variance = jnp.mean(centred * centred, axis=-1, keepdims=True)
        normed[pl.ds(t * 128, 128), :] = (centred * lax.rsqrt(variance + EPS)).astype(BF16)

    def turn_weights(u):
        for k in range(4):
            wt[u, k] = win[u, :, k * 128 : (k + 1) * 128].astype(F32).T.astype(BF16)

    def project(step, update):
        dx, dh = far_first(step)
        chip = lax.rem(x + dx, 4) * 2 + lax.rem(yh + dh, 2)
        at = pl.ds(pl.multiple_of(chip * 16, 16), 16)
        w = jnp.concatenate([wt[update, k, at, :] for k in range(4)], axis=0)
        p = lax.dot_general(w, normed[...], (((1,), (1,)), ((), ())), preferred_element_type=F32)
        both = []
        for k in (0, 32):
            side = sigmoid(p[k + 16 : k + 32]) * p[k : k + 16]
            tiles = jnp.stack([side[:, t * 128 : (t + 1) * 128] for t in range(8)], axis=0)
            both.append(jnp.swapaxes(tiles, 0, 1) * mask8[...][None])
        send1[update, at] = jnp.concatenate(both, axis=1).astype(BF16)

    for t in range(8):
        loads[t].wait()
        normalize_rows(t, zp[t].reshape(128, 128).astype(F32))
    loads[8].wait()
    turn_weights(0)

    for update in range(2):
        half = y if update == 0 else c // 8
        corner = lax.rem(c, 4)
        slot = x * 32 + z * 4 + corner if update == 0 else lax.rem(x, 2) * 64 + r * 4 + corner
        own = half == core

        def spread(step, update=update, half=half, own=own, slot=slot):
            dx, dh = far_first(step)
            chip = lax.rem(x + dx, 4) * 2 + lax.rem(yh + dh, 2)

            def send(row):
                pltpu.make_async_remote_copy(
                    src_ref=send1.at[update, chip * 16 + row],
                    dst_ref=recv1.at[update, slot],
                    send_sem=sem1s.at[update],
                    recv_sem=sem1r.at[update, dx],
                    device_id=(row, chip * 2 + half),
                    device_id_type=MESH,
                ).start()

            near = lax.rem(y + dh, 2)
            for parity, line in ((0, 1 - near), (0, near), (1, 1 - near), (1, near)):
                odd = lax.rem(parity + line + z + chip // 2 + chip, 2) == 1
                for way, dz in enumerate(ALONG_Z):
                    row = line * 8 + lax.rem(z + jnp.where(odd, dz[1], dz[0]), 8)
                    if way < 3 or line is not near:
                        send(row)
                        continue
                    here = (step == 7) & own & jnp.logical_not(odd)

                    @pl.when(jnp.logical_not(here))
                    def _(row=row):
                        send(row)

                    @pl.when(here)
                    def _():
                        pltpu.make_async_copy(
                            send1.at[update, me], recv1.at[update, slot], sem1r.at[update, dx]
                        ).start()

        if update == 0:
            project(0, 0)
            pl.semaphore_wait(barrier, 23)

            def tell(step, carry):
                dx, dh = far_first(step)
                peer = lax.rem(x + 6 - dx, 4) * 4 + lax.rem(1 + yh + dh, 2) * 2 + core
                pl.semaphore_signal(ready.at[step], inc=1, device_id=(r, peer), device_id_type=MESH)
                return carry

            lax.fori_loop(1, 8, tell, 0)
            spread(0)

            @pl.loop(1, 8)
            def _(step, spread=spread):
                project(step, 0)
                pl.semaphore_wait(ready.at[step], 1)
                spread(step)

        else:

            @pl.loop(0, 8)
            def _(step, spread=spread):
                project(step, 1)
                spread(step)

        if update == 0:
            turn_weights(1)
            loads[9].wait()
            loads[10].wait()

        @pl.loop(0, 4)
        def _(i, update=update):
            at = pl.ds(pl.multiple_of(i * 256, 256), 256)
            gate[at, :] = sigmoid(jnp.dot(normed[at, :], wgate[update], preferred_element_type=F32))

        left, right = (left0, right0) if update == 0 else (left1, right1)
        columns = 4 if update == 0 else 2
        count = 128 // columns

        def arrive(dx, update=update, left=left, right=right, columns=columns, count=count):
            k = lax.rem(x + 4 - dx, columns)
            got = recv1.at[update, pl.ds(0, count)]
            pltpu.make_async_copy(got, got, sem1r.at[update, dx]).wait()
            for part in range(count // 32):
                at = pl.ds(part * 256, 256)
                v = recv1[update, pl.ds(k * count + part * 32, 32)].astype(F32).reshape(8, 4, 16, 128)
                parts = swap_blocks([v[:, q] for q in range(4)])
                for side in range(2):
                    rows = jnp.stack([p[:, side * 8 : side * 8 + 8] for p in parts], axis=1)
                    rows = rows.reshape(256, 128).astype(BF16)
                    if side == 0:
                        left[k, at, :] = rows
                    else:
                        right[core, k, at, :] = rows
            part = right.at[core, k]
            pltpu.make_async_remote_copy(
                src_ref=part, dst_ref=part, send_sem=semxs.at[update], recv_sem=semxr.at[update],
                device_id=sibling, device_id_type=MESH,
            ).start()

        if update == 0:

            def each(i, carry, arrive=arrive):
                arrive(jnp.where(i == 0, 2, jnp.where(i == 3, 0, 2 * i - 1)))
                return carry

            lax.fori_loop(0, 4, each, 0)
        else:
            ways = lax.rem(x + 4 - core * 2, 4)
            other = lax.rem(ways + 3, 4)
            even, odd = jnp.where(lax.rem(ways, 2) == 0, ways, other), jnp.where(lax.rem(ways, 2) == 0, other, ways)
            arrive(jnp.where(even == 2, even, odd))
            arrive(jnp.where(even == 2, odd, even))
        own_back = y == core
        way = lax.rem(core * 2 + 4 - x, 4)
        own_far = (way == 2) | (way == 1)
        own_odd = jnp.where(lax.rem(way, 2) == 1, way, lax.rem(way + 1, 4))

        def block_of(i, own_far=own_far, own_odd=own_odd):
            first = jnp.where(own_far, 2, own_odd)
            second = jnp.where(own_far, own_odd, 2)
            dx = jnp.where(i == 0, first, jnp.where(i == 1, second, jnp.where(i == 2, 4 - own_odd, 0)))
            return lax.rem(x + dx, 4)

        def back_sends(i, update=update, block_of=block_of, own_back=own_back):
            k = block_of(i)

            def send(col, b):
                pltpu.make_async_remote_copy(
                    src_ref=send2.at[update, col * 8 + b],
                    dst_ref=recv2.at[update, me],
                    send_sem=sem2s.at[update],
                    recv_sem=sem2r.at[update],
                    device_id=(core * 8 + b, col),
                    device_id_type=MESH,
                ).start()

            for parity, h in ((0, 1 - yh), (0, yh), (1, 1 - yh), (1, yh)):
                odd = lax.rem(parity + core + z + k + h, 2) == 1
                for way, dz in enumerate(ALONG_Z):
                    b = lax.rem(z + jnp.where(odd, dz[1], dz[0]), 8)
                    send(k * 4 + h * 2 + 1 - core, b)
                    if way < 3 or h is not yh:
                        send(k * 4 + h * 2 + core, b)
                        continue
                    here = (i == 3) & own_back & jnp.logical_not(odd)

                    @pl.when(jnp.logical_not(here))
                    def _(h=h, b=b):
                        send(k * 4 + h * 2 + core, b)

                    @pl.when(here)
                    def _():
                        pltpu.make_async_copy(
                            send2.at[update, c * 8 + z], recv2.at[update, me], sem2r.at[update]
                        ).start()

        def back(i, carry, update=update, left=left, right=right, block_of=block_of, back_sends=back_sends):
            k = block_of(i)
            if update == 0:
                some = pl.ds(pl.multiple_of(lax.rem(k, 2) * 128, 128), 128)
                lhs = jnp.concatenate([left[q] for q in range(4)], axis=1)
                rhs = jnp.concatenate([right[k // 2, q, some, :] for q in range(4)], axis=1)
                v = lax.dot_general(lhs, rhs, (((1,), (1,)), ((), ())), preferred_element_type=F32)
            else:
                lhs = jnp.concatenate([left[q] for q in range(2)], axis=1)
                rhs = right[k // 2, lax.rem(k, 2)]
                v = lax.dot_general(lhs, rhs, (((0,), (0,)), ((), ())), preferred_element_type=F32)
            v = v.reshape(8, 4, 8, 128)
            parts = swap_blocks([v[:, u] for u in range(4)])
            for q in range(4):
                send2[update, pl.ds((k * 4 + q) * 8, 8)] = parts[q].astype(BF16)

            back_sends(i)
            return carry

        back(0, 0)
        theirs = right.at[1 - core]
        pltpu.make_async_copy(theirs, theirs, semxr.at[update]).wait()
        lax.fori_loop(1, 4, back, 0)
        pltpu.make_async_copy(recv2.at[update], recv2.at[update], sem2r.at[update]).wait()

        tiles = jnp.swapaxes(recv2[update].astype(F32), 0, 1)
        for t in range(8):
            v = tiles[t]
            centred = v - jnp.mean(v, axis=0, keepdims=True)
            variance = jnp.mean(centred * centred, axis=0, keepdims=True)
            v = (centred * lax.rsqrt(variance + EPS)).astype(BF16)
            term = lax.dot_general(v, wout[update], (((0,), (0,)), ((), ())), preferred_element_type=F32)
            at = pl.ds(t * 128, 128)
            new = zp[t].reshape(128, 128).astype(F32) + gate[at, :] * term
            if update == 0:
                new = new.astype(BF16)
                zp[t] = new.reshape(4, 32, 128)
                normalize_rows(t, new.astype(F32))
            else:
                for u in range(4):
                    out_ref[u * 8 + t] = new[u * 32 : u * 32 + 32].astype(BF16)

        mine = right.at[core]
        pltpu.make_async_copy(mine, mine, semxs.at[update]).wait()
        for sent, sem, all_remote, count in (
            (send1, sem1s, jnp.logical_not(own), 128),
            (send2, sem2s, jnp.logical_not(own_back), 128),
        ):

            @pl.when(all_remote)
            def _(update=update, sent=sent, sem=sem):
                pltpu.make_async_copy(sent.at[update], sent.at[update], sem.at[update]).wait()

            @pl.when(jnp.logical_not(all_remote))
            def _(update=update, sent=sent, sem=sem, count=count):
                gone = sent.at[update, pl.ds(0, count - 1)]
                pltpu.make_async_copy(gone, gone, sem.at[update]).wait()


def per_device(pair_rep, residue_mask, input_weights, gate_weights, output_weights):
    vmem = pl.BlockSpec(memory_space=pltpu.VMEM)
    anywhere = pl.BlockSpec(memory_space=pl.ANY)
    dma = pltpu.SemaphoreType.DMA((2,))
    out = pl.pallas_call(
        kernel,
        out_shape=jax.ShapeDtypeStruct((32, 32, 128), BF16),
        in_specs=[anywhere] * 5,
        out_specs=vmem,
        scratch_shapes=[
            pltpu.VMEM((8, 4, 32, 128), BF16),
            pltpu.VMEM((1, 512), jnp.int32),
            pltpu.VMEM((2, 128, 512), BF16),
            pltpu.VMEM((2, 128, 128), BF16),
            pltpu.VMEM((2, 128, 128), BF16),
            pltpu.VMEM((1024, 128), BF16),
            pltpu.VMEM((2, 4, 128, 128), BF16),
            pltpu.VMEM((8, 128), F32),
            pltpu.VMEM((1024, 128), F32),
            pltpu.VMEM((2, 128, 16, 128), BF16),
            pltpu.VMEM((2, 128, 16, 128), BF16),
            pltpu.VMEM((4, 256, 128), BF16),
            pltpu.VMEM((2, 4, 256, 128), BF16),
            pltpu.VMEM((2, 512, 128), BF16),
            pltpu.VMEM((2, 2, 512, 128), BF16),
            pltpu.VMEM((2, 128, 8, 128), BF16),
            pltpu.VMEM((2, 128, 8, 128), BF16),
            pltpu.SemaphoreType.DMA((12,)),
            dma, pltpu.SemaphoreType.DMA((2, 4)), dma, dma, dma, dma,
            pltpu.SemaphoreType.REGULAR((8,)),
        ],
        compiler_params=pltpu.CompilerParams(
            collective_id=0, has_side_effects=True, vmem_limit_bytes=32 * 1024 * 1024
        ),
        name="triangles",
    )(
        pltpu.with_memory_space_constraint(pair_rep.reshape(4, 8, 32, 128), pltpu.HBM),
        pltpu.with_memory_space_constraint(residue_mask.reshape(1, 512), pltpu.HBM),
        pltpu.with_memory_space_constraint(input_weights, pltpu.HBM),
        pltpu.with_memory_space_constraint(gate_weights, pltpu.HBM),
        pltpu.with_memory_space_constraint(output_weights, pltpu.HBM),
    )
    return out


def solution(mesh):
    placed = (P("row", "col", None), P(), P(), P(), P())
    return jax.shard_map(
        per_device, mesh=mesh, in_specs=placed, out_specs=P("row", "col", None), check_vma=False
    )
```

```python
import functools

import jax
import jax.numpy as jnp
from jax import lax
from jax.experimental import pallas as pl
from jax.experimental.pallas import tpu as pltpu
from jax.sharding import PartitionSpec as P

EPS = 1e-05
MESH = pl.DeviceIdType.MESH
F32 = jnp.float32
BF16 = jnp.bfloat16


def sigmoid(x):
    return 0.5 * jnp.tanh(0.5 * x) + 0.5


def swap_blocks(parts):
    group = lax.broadcasted_iota(jnp.int32, parts[0].shape, parts[0].ndim - 1) // 32
    axis = parts[0].ndim - 1
    high = group >= 2
    odd = lax.rem(group, 2) == 1

    def far(a, b):
        c = pltpu.roll(jnp.where(high, a, b), 64, axis)
        return jnp.where(high, c, a), jnp.where(high, b, c)

    def near(a, b):
        c = jnp.where(odd, a, b)
        return jnp.where(odd, pltpu.roll(c, 32, axis), a), jnp.where(odd, b, pltpu.roll(c, 96, axis))

    p0, p2 = far(parts[0], parts[2])
    p1, p3 = far(parts[1], parts[3])
    p0, p1 = near(p0, p1)
    p2, p3 = near(p2, p3)
    return p0, p1, p2, p3


def far_first(step):
    pair, second = step // 2, lax.rem(step, 2)
    middle = (pair == 1) | (pair == 2)
    dx = jnp.where(middle, 1 + 2 * second, jnp.where(pair == 0, 2, 0))
    return dx, jnp.where(middle, 2 - pair, 1 - second)


ALONG_Z = ((4, 3), (2, 5), (6, 1), (0, 7))


def kernel(
    z_hbm, mask_hbm, win_hbm, wgate_hbm, wout_hbm, out_ref,
    zp, mask_ref, win, wgate, wout, normed, wt, mask8, gate,
    send1, recv1, left0, right0, left1, right1, send2, recv2,
    load, sem1s, sem1r, semxs, semxr, sem2s, sem2r, ready,
):
    r, c = lax.axis_index("row"), lax.axis_index("col")
    cc, core = c // 2, lax.rem(c, 2)
    y, z = r // 8, lax.rem(r, 8)
    x, yh = cc // 2, lax.rem(cc, 2)
    me = cc * 16 + r
    sibling = (r, cc * 2 + 1 - core)

    loads = [pltpu.make_async_copy(z_hbm.at[:, t], zp.at[t], load.at[t]) for t in range(8)]
    loads.append(pltpu.make_async_copy(win_hbm, win, load.at[8]))
    loads.append(pltpu.make_async_copy(wgate_hbm, wgate, load.at[9]))
    loads.append(pltpu.make_async_copy(wout_hbm, wout, load.at[10]))
    loads.append(pltpu.make_async_copy(mask_hbm, mask_ref, load.at[11]))
    for one in loads:
        one.start()

    barrier = pltpu.get_barrier_semaphore()

    for dz in (4, 3, 5, 2, 6, 1, 7, 0):
        row = core * 8 + lax.rem(z + dz, 8)
        for k in range(2):
            far = lax.rem(x + 2, 4) * 4 + (1 - yh) * 2 + k
            pl.semaphore_signal(barrier, inc=1, device_id=(row, far), device_id_type=MESH)

    @pl.loop(1, 8)
    def _(t):
        peer = lax.rem(cc + t, 8) * 2 + core
        pl.semaphore_signal(barrier, inc=1, device_id=(r, peer), device_id_type=MESH)

    n8 = lax.broadcasted_iota(jnp.int32, (8, 512), 1)
    t8 = lax.broadcasted_iota(jnp.int32, (8, 512), 0)
    n = lax.broadcasted_iota(jnp.int32, (512, 128), 0)
    l = lax.broadcasted_iota(jnp.int32, (512, 128), 1)
    pick_row = jnp.where(n // 8 == 4 * r + l // 32, 1.0, 0.0).astype(BF16)
    pick_col = jnp.where(n == 32 * c + lax.rem(l, 32), 1.0, 0.0).astype(BF16)
    loads[11].wait()
    valid = jnp.broadcast_to(mask_ref[...].astype(F32), (8, 512))
    rows = jnp.where(lax.rem(n8, 8) == t8, valid, 0.0).astype(BF16)
    mask8[...] = jnp.dot(rows, pick_row, preferred_element_type=F32) * jnp.dot(
        valid.astype(BF16), pick_col, preferred_element_type=F32
    )

    def normalize_rows(t, v):
        centred = v - jnp.mean(v, axis=-1, keepdims=True)
        variance = jnp.mean(centred * centred, axis=-1, keepdims=True)
        normed[pl.ds(t * 128, 128), :] = (centred * lax.rsqrt(variance + EPS)).astype(BF16)

    def turn_weights(u):
        for k in range(4):
            wt[u, k] = win[u, :, k * 128 : (k + 1) * 128].astype(F32).T.astype(BF16)

    def project(step, update):
        dx, dh = far_first(step)
        chip = lax.rem(x + dx, 4) * 2 + lax.rem(yh + dh, 2)
        at = pl.ds(pl.multiple_of(chip * 16, 16), 16)
        w = jnp.concatenate([wt[update, k, at, :] for k in range(4)], axis=0)
        p = lax.dot_general(w, normed[...], (((1,), (1,)), ((), ())), preferred_element_type=F32)
        both = []
        for k in (0, 32):
            side = sigmoid(p[k + 16 : k + 32]) * p[k : k + 16]
            tiles = jnp.stack([side[:, t * 128 : (t + 1) * 128] for t in range(8)], axis=0)
            both.append(jnp.swapaxes(tiles, 0, 1) * mask8[...][None])
        send1[update, at] = jnp.concatenate(both, axis=1).astype(BF16)

    def all_left(sent, sem, update, own):
        @pl.when(own)
        def _():
            some = sent.at[update, pl.ds(0, 127)]
            pltpu.make_async_copy(some, some, sem.at[update]).wait()

        @pl.when(jnp.logical_not(own))
        def _():
            pltpu.make_async_copy(sent.at[update], sent.at[update], sem.at[update]).wait()

    for t in range(8):
        loads[t].wait()
    for t in range(8):
        normalize_rows(t, zp[t].reshape(128, 128).astype(F32))
    loads[8].wait()
    turn_weights(0)

    for update in range(2):
        half = y if update == 0 else c // 8
        corner = lax.rem(c, 4)
        slot = x * 32 + z * 4 + corner if update == 0 else lax.rem(x, 2) * 64 + r * 4 + corner
        own = half == core

        def spread(step, update=update, half=half, own=own, slot=slot):
            dx, dh = far_first(step)
            chip = lax.rem(x + dx, 4) * 2 + lax.rem(yh + dh, 2)

            def send(row):
                pltpu.make_async_remote_copy(
                    src_ref=send1.at[update, chip * 16 + row],
                    dst_ref=recv1.at[update, slot],
                    send_sem=sem1s.at[update],
                    recv_sem=sem1r.at[update, dx],
                    device_id=(row, chip * 2 + half),
                    device_id_type=MESH,
                ).start()

            near = lax.rem(y + dh, 2)
            for parity, line in ((0, 1 - near), (0, near), (1, 1 - near), (1, near)):
                odd = lax.rem(parity + line + z + chip // 2 + chip, 2) == 1
                for way, dz in enumerate(ALONG_Z):
                    row = line * 8 + lax.rem(z + jnp.where(odd, dz[1], dz[0]), 8)
                    if way < 3 or line is not near:
                        send(row)
                        continue
                    here = (step == 7) & own & jnp.logical_not(odd)

                    @pl.when(jnp.logical_not(here))
                    def _(row=row):
                        send(row)

                    @pl.when(here)
                    def _():
                        pltpu.make_async_copy(
                            send1.at[update, me], recv1.at[update, slot], sem1r.at[update, dx]
                        ).start()

        if update == 0:
            project(0, 0)
            pl.semaphore_wait(barrier, 23)

            def tell(step, carry):
                dx, dh = far_first(step)
                peer = lax.rem(x + 6 - dx, 4) * 4 + lax.rem(1 + yh + dh, 2) * 2 + core
                pl.semaphore_signal(ready.at[step], inc=1, device_id=(r, peer), device_id_type=MESH)
                return carry

            lax.fori_loop(1, 8, tell, 0)
            spread(0)

            @pl.loop(1, 8)
            def _(step, spread=spread):
                project(step, 0)
                pl.semaphore_wait(ready.at[step], 1)
                spread(step)

        else:

            @pl.loop(0, 8)
            def _(step, spread=spread):
                project(step, 1)
                spread(step)

        if update == 0:
            turn_weights(1)
            loads[9].wait()
            loads[10].wait()

        @pl.loop(0, 4)
        def _(i, update=update):
            at = pl.ds(pl.multiple_of(i * 256, 256), 256)
            gate[at, :] = sigmoid(jnp.dot(normed[at, :], wgate[update], preferred_element_type=F32))

        left, right = (left0, right0) if update == 0 else (left1, right1)
        columns = 4 if update == 0 else 2
        count = 128 // columns

        def arrive(dx, update=update, left=left, right=right, columns=columns, count=count):
            k = lax.rem(x + 4 - dx, columns)
            got = recv1.at[update, pl.ds(0, count)]
            pltpu.make_async_copy(got, got, sem1r.at[update, dx]).wait()
            for part in range(count // 32):
                at = pl.ds(part * 256, 256)
                v = recv1[update, pl.ds(k * count + part * 32, 32)].astype(F32).reshape(8, 4, 16, 128)
                parts = swap_blocks([v[:, q] for q in range(4)])
                for side in range(2):
                    rows = jnp.stack([p[:, side * 8 : side * 8 + 8] for p in parts], axis=1)
                    rows = rows.reshape(256, 128).astype(BF16)
                    if side == 0:
                        left[k, at, :] = rows
                    else:
                        right[core, k, at, :] = rows
            part = right.at[core, k]
            pltpu.make_async_remote_copy(
                src_ref=part, dst_ref=part, send_sem=semxs.at[update], recv_sem=semxr.at[update],
                device_id=sibling, device_id_type=MESH,
            ).start()

        if update == 0:

            def each(i, carry, arrive=arrive):
                arrive(jnp.where(i == 0, 2, jnp.where(i == 3, 0, 2 * i - 1)))
                return carry

            lax.fori_loop(0, 4, each, 0)
        else:
            ways = lax.rem(x + 4 - core * 2, 4)
            other = lax.rem(ways + 3, 4)
            even, odd = jnp.where(lax.rem(ways, 2) == 0, ways, other), jnp.where(lax.rem(ways, 2) == 0, other, ways)
            arrive(jnp.where(even == 2, even, odd))
            arrive(jnp.where(even == 2, odd, even))
        own_back = y == core
        way = lax.rem(core * 2 + 4 - x, 4)
        own_far = (way == 2) | (way == 1)
        own_odd = jnp.where(lax.rem(way, 2) == 1, way, lax.rem(way + 1, 4))

        def block_of(i, own_far=own_far, own_odd=own_odd):
            first = jnp.where(own_far, 2, own_odd)
            second = jnp.where(own_far, own_odd, 2)
            dx = jnp.where(i == 0, first, jnp.where(i == 1, second, jnp.where(i == 2, 4 - own_odd, 0)))
            return lax.rem(x + dx, 4)

        def back_sends(i, update=update, block_of=block_of, own_back=own_back):
            k = block_of(i)

            def send(col, b):
                pltpu.make_async_remote_copy(
                    src_ref=send2.at[update, col * 8 + b],
                    dst_ref=recv2.at[update, me],
                    send_sem=sem2s.at[update],
                    recv_sem=sem2r.at[update],
                    device_id=(core * 8 + b, col),
                    device_id_type=MESH,
                ).start()

            for parity, h in ((0, 1 - yh), (0, yh), (1, 1 - yh), (1, yh)):
                odd = lax.rem(parity + core + z + k + h, 2) == 1
                for way, dz in enumerate(ALONG_Z):
                    b = lax.rem(z + jnp.where(odd, dz[1], dz[0]), 8)
                    send(k * 4 + h * 2 + 1 - core, b)
                    if way < 3 or h is not yh:
                        send(k * 4 + h * 2 + core, b)
                        continue
                    here = (i == 3) & own_back & jnp.logical_not(odd)

                    @pl.when(jnp.logical_not(here))
                    def _(h=h, b=b):
                        send(k * 4 + h * 2 + core, b)

                    @pl.when(here)
                    def _():
                        pltpu.make_async_copy(
                            send2.at[update, c * 8 + z], recv2.at[update, me], sem2r.at[update]
                        ).start()

        def back(i, carry, update=update, left=left, right=right, block_of=block_of, back_sends=back_sends):
            k = block_of(i)
            if update == 0:
                some = pl.ds(pl.multiple_of(lax.rem(k, 2) * 128, 128), 128)
                lhs = jnp.concatenate([left[q] for q in range(4)], axis=1)
                rhs = jnp.concatenate([right[k // 2, q, some, :] for q in range(4)], axis=1)
                v = lax.dot_general(lhs, rhs, (((1,), (1,)), ((), ())), preferred_element_type=F32)
            else:
                lhs = jnp.concatenate([left[q] for q in range(2)], axis=1)
                rhs = right[k // 2, lax.rem(k, 2)]
                v = lax.dot_general(lhs, rhs, (((0,), (0,)), ((), ())), preferred_element_type=F32)
            v = v.reshape(8, 4, 8, 128)
            parts = swap_blocks([v[:, u] for u in range(4)])
            for q in range(4):
                send2[update, pl.ds((k * 4 + q) * 8, 8)] = parts[q].astype(BF16)

            back_sends(i)
            return carry

        back(0, 0)
        theirs = right.at[1 - core]
        pltpu.make_async_copy(theirs, theirs, semxr.at[update]).wait()
        lax.fori_loop(1, 4, back, 0)
        mine = right.at[core]
        pltpu.make_async_copy(mine, mine, semxs.at[update]).wait()
        all_left(send1, sem1s, update, own)
        pltpu.make_async_copy(recv2.at[update], recv2.at[update], sem2r.at[update]).wait()

        tiles = jnp.swapaxes(recv2[update].astype(F32), 0, 1)
        for t in range(8):
            v = tiles[t]
            centred = v - jnp.mean(v, axis=0, keepdims=True)
            variance = jnp.mean(centred * centred, axis=0, keepdims=True)
            v = (centred * lax.rsqrt(variance + EPS)).astype(BF16)
            term = lax.dot_general(v, wout[update], (((0,), (0,)), ((), ())), preferred_element_type=F32)
            at = pl.ds(t * 128, 128)
            new = zp[t].reshape(128, 128).astype(F32) + gate[at, :] * term
            if update == 0:
                new = new.astype(BF16)
                zp[t] = new.reshape(4, 32, 128)
                normalize_rows(t, new.astype(F32))
            else:
                for u in range(4):
                    out_ref[u * 8 + t] = new[u * 32 : u * 32 + 32].astype(BF16)

    own_back = y == core
    for update in range(2):
        all_left(send2, sem2s, update, own_back)


def per_device(pair_rep, residue_mask, input_weights, gate_weights, output_weights):
    vmem = pl.BlockSpec(memory_space=pltpu.VMEM)
    anywhere = pl.BlockSpec(memory_space=pl.ANY)
    dma = pltpu.SemaphoreType.DMA((2,))
    out = pl.pallas_call(
        kernel,
        out_shape=jax.ShapeDtypeStruct((32, 32, 128), BF16),
        in_specs=[anywhere] * 5,
        out_specs=vmem,
        scratch_shapes=[
            pltpu.VMEM((8, 4, 32, 128), BF16),
            pltpu.VMEM((1, 512), jnp.int32),
            pltpu.VMEM((2, 128, 512), BF16),
            pltpu.VMEM((2, 128, 128), BF16),
            pltpu.VMEM((2, 128, 128), BF16),
            pltpu.VMEM((1024, 128), BF16),
            pltpu.VMEM((2, 4, 128, 128), BF16),
            pltpu.VMEM((8, 128), F32),
            pltpu.VMEM((1024, 128), F32),
            pltpu.VMEM((2, 128, 16, 128), BF16),
            pltpu.VMEM((2, 128, 16, 128), BF16),
            pltpu.VMEM((4, 256, 128), BF16),
            pltpu.VMEM((2, 4, 256, 128), BF16),
            pltpu.VMEM((2, 512, 128), BF16),
            pltpu.VMEM((2, 2, 512, 128), BF16),
            pltpu.VMEM((2, 128, 8, 128), BF16),
            pltpu.VMEM((2, 128, 8, 128), BF16),
            pltpu.SemaphoreType.DMA((12,)),
            dma, pltpu.SemaphoreType.DMA((2, 4)), dma, dma, dma, dma,
            pltpu.SemaphoreType.REGULAR((8,)),
        ],
        compiler_params=pltpu.CompilerParams(
            collective_id=0, has_side_effects=True, vmem_limit_bytes=32 * 1024 * 1024
        ),
        name="triangles",
    )(
        pltpu.with_memory_space_constraint(pair_rep.reshape(4, 8, 32, 128), pltpu.HBM),
        pltpu.with_memory_space_constraint(residue_mask.reshape(1, 512), pltpu.HBM),
        pltpu.with_memory_space_constraint(input_weights, pltpu.HBM),
        pltpu.with_memory_space_constraint(gate_weights, pltpu.HBM),
        pltpu.with_memory_space_constraint(output_weights, pltpu.HBM),
    )
    return out


def solution(mesh):
    placed = (P("row", "col", None), P(), P(), P(), P())
    return jax.shard_map(
        per_device, mesh=mesh, in_specs=placed, out_specs=P("row", "col", None), check_vma=False
    )
```

```python
import functools

import jax
import jax.numpy as jnp
from jax import lax
from jax.experimental import pallas as pl
from jax.experimental.pallas import tpu as pltpu
from jax.sharding import PartitionSpec as P

EPS = 1e-05
MESH = pl.DeviceIdType.MESH
F32 = jnp.float32
BF16 = jnp.bfloat16


def sigmoid(x):
    return 0.5 * jnp.tanh(0.5 * x) + 0.5


def swap_blocks(parts):
    group = lax.broadcasted_iota(jnp.int32, parts[0].shape, parts[0].ndim - 1) // 32
    axis = parts[0].ndim - 1
    high = group >= 2
    odd = lax.rem(group, 2) == 1

    def far(a, b):
        c = pltpu.roll(jnp.where(high, a, b), 64, axis)
        return jnp.where(high, c, a), jnp.where(high, b, c)

    def near(a, b):
        c = jnp.where(odd, a, b)
        return jnp.where(odd, pltpu.roll(c, 32, axis), a), jnp.where(odd, b, pltpu.roll(c, 96, axis))

    p0, p2 = far(parts[0], parts[2])
    p1, p3 = far(parts[1], parts[3])
    p0, p1 = near(p0, p1)
    p2, p3 = near(p2, p3)
    return p0, p1, p2, p3


def far_first(step):
    pair, second = step // 2, lax.rem(step, 2)
    middle = (pair == 1) | (pair == 2)
    dx = jnp.where(middle, 1 + 2 * second, jnp.where(pair == 0, 2, 0))
    return dx, jnp.where(middle, 2 - pair, 1 - second)


ALONG_Z = ((4, 3), (2, 5), (6, 1), (0, 7))


def kernel(
    z_hbm, mask_hbm, win_hbm, wgate_hbm, wout_hbm, out_ref,
    zp, mask_ref, win, wgate, wout, normed, wt, mask8, gate,
    send1, recv1, left0, right0, left1, right1, send2, recv2,
    load, sem1s, sem1r, semxs, semxr, sem2s, sem2r, ready,
):
    r, c = lax.axis_index("row"), lax.axis_index("col")
    cc, core = c // 2, lax.rem(c, 2)
    y, z = r // 8, lax.rem(r, 8)
    x, yh = cc // 2, lax.rem(cc, 2)
    me = cc * 16 + r
    sibling = (r, cc * 2 + 1 - core)

    loads = [pltpu.make_async_copy(z_hbm.at[:, t], zp.at[t], load.at[t]) for t in range(8)]
    loads.append(pltpu.make_async_copy(win_hbm, win, load.at[8]))
    loads.append(pltpu.make_async_copy(wgate_hbm, wgate, load.at[9]))
    loads.append(pltpu.make_async_copy(wout_hbm, wout, load.at[10]))
    loads.append(pltpu.make_async_copy(mask_hbm, mask_ref, load.at[11]))
    for one in loads:
        one.start()

    barrier = pltpu.get_barrier_semaphore()

    for dz in (4, 3, 5, 2, 6, 1, 7, 0):
        row = core * 8 + lax.rem(z + dz, 8)
        for k in range(2):
            far = lax.rem(x + 2, 4) * 4 + (1 - yh) * 2 + k
            pl.semaphore_signal(barrier, inc=1, device_id=(row, far), device_id_type=MESH)

    @pl.loop(1, 8)
    def _(t):
        peer = lax.rem(cc + t, 8) * 2 + core
        pl.semaphore_signal(barrier, inc=1, device_id=(r, peer), device_id_type=MESH)

    n8 = lax.broadcasted_iota(jnp.int32, (8, 512), 1)
    t8 = lax.broadcasted_iota(jnp.int32, (8, 512), 0)
    n = lax.broadcasted_iota(jnp.int32, (512, 128), 0)
    l = lax.broadcasted_iota(jnp.int32, (512, 128), 1)
    pick_row = jnp.where(n // 8 == 4 * r + l // 32, 1.0, 0.0).astype(BF16)
    pick_col = jnp.where(n == 32 * c + lax.rem(l, 32), 1.0, 0.0).astype(BF16)
    loads[11].wait()
    valid = jnp.broadcast_to(mask_ref[...].astype(F32), (8, 512))
    rows = jnp.where(lax.rem(n8, 8) == t8, valid, 0.0).astype(BF16)
    mask8[...] = jnp.dot(rows, pick_row, preferred_element_type=F32) * jnp.dot(
        valid.astype(BF16), pick_col, preferred_element_type=F32
    )

    def normalize_rows(t, v):
        centred = v - jnp.mean(v, axis=-1, keepdims=True)
        variance = jnp.mean(centred * centred, axis=-1, keepdims=True)
        normed[pl.ds(t * 128, 128), :] = (centred * lax.rsqrt(variance + EPS)).astype(BF16)

    def turn_weights(u):
        for k in range(4):
            wt[u, k] = win[u, :, k * 128 : (k + 1) * 128].astype(F32).T.astype(BF16)

    def project(step, update):
        dx, dh = far_first(step)
        chip = lax.rem(x + dx, 4) * 2 + lax.rem(yh + dh, 2)
        at = pl.ds(pl.multiple_of(chip * 16, 16), 16)
        w = jnp.concatenate([wt[update, k, at, :] for k in range(4)], axis=0)
        p = lax.dot_general(w, normed[...], (((1,), (1,)), ((), ())), preferred_element_type=F32)
        both = []
        for k in (0, 32):
            side = sigmoid(p[k + 16 : k + 32]) * p[k : k + 16]
            tiles = jnp.stack([side[:, t * 128 : (t + 1) * 128] for t in range(8)], axis=0)
            both.append(jnp.swapaxes(tiles, 0, 1) * mask8[...][None])
        send1[update, at] = jnp.concatenate(both, axis=1).astype(BF16)

    for t in range(8):
        loads[t].wait()
        normalize_rows(t, zp[t].reshape(128, 128).astype(F32))
    loads[8].wait()
    turn_weights(0)

    for update in range(2):
        half = y if update == 0 else c // 8
        corner = lax.rem(c, 4)
        slot = x * 32 + z * 4 + corner if update == 0 else lax.rem(x, 2) * 64 + r * 4 + corner
        own = half == core

        def spread(step, update=update, half=half, own=own, slot=slot):
            dx, dh = far_first(step)
            chip = lax.rem(x + dx, 4) * 2 + lax.rem(yh + dh, 2)

            def send(row):
                pltpu.make_async_remote_copy(
                    src_ref=send1.at[update, chip * 16 + row],
                    dst_ref=recv1.at[update, slot],
                    send_sem=sem1s.at[update],
                    recv_sem=sem1r.at[update, dx],
                    device_id=(row, chip * 2 + half),
                    device_id_type=MESH,
                ).start()

            near = lax.rem(y + dh, 2)
            for parity, line in ((0, 1 - near), (0, near), (1, 1 - near), (1, near)):
                odd = lax.rem(parity + line + z + chip // 2 + chip, 2) == 1
                for way, dz in enumerate(ALONG_Z):
                    row = line * 8 + lax.rem(z + jnp.where(odd, dz[1], dz[0]), 8)
                    if way < 3 or line is not near:
                        send(row)
                        continue
                    here = (step == 7) & own & jnp.logical_not(odd)

                    @pl.when(jnp.logical_not(here))
                    def _(row=row):
                        send(row)

                    @pl.when(here)
                    def _():
                        pltpu.make_async_copy(
                            send1.at[update, me], recv1.at[update, slot], sem1r.at[update, dx]
                        ).start()

        if update == 0:
            project(0, 0)
            pl.semaphore_wait(barrier, 23)

            def tell(step, carry):
                dx, dh = far_first(step)
                peer = lax.rem(x + 6 - dx, 4) * 4 + lax.rem(1 + yh + dh, 2) * 2 + core
                pl.semaphore_signal(ready.at[step], inc=1, device_id=(r, peer), device_id_type=MESH)
                return carry

            lax.fori_loop(1, 8, tell, 0)
            spread(0)

            @pl.loop(1, 8)
            def _(step, spread=spread):
                project(step, 0)
                pl.semaphore_wait(ready.at[step], 1)
                spread(step)

        else:

            @pl.loop(0, 8)
            def _(step, spread=spread):
                project(step, 1)
                spread(step)

        if update == 0:
            turn_weights(1)
            loads[9].wait()
            loads[10].wait()

        @pl.loop(0, 4)
        def _(i, update=update):
            at = pl.ds(pl.multiple_of(i * 256, 256), 256)
            gate[at, :] = sigmoid(jnp.dot(normed[at, :], wgate[update], preferred_element_type=F32))

        left, right = (left0, right0) if update == 0 else (left1, right1)
        columns = 4 if update == 0 else 2
        count = 128 // columns

        def arrive(dx, update=update, left=left, right=right, columns=columns, count=count):
            k = lax.rem(x + 4 - dx, columns)
            got = recv1.at[update, pl.ds(0, count)]
            pltpu.make_async_copy(got, got, sem1r.at[update, dx]).wait()
            for part in range(count // 32):
                at = pl.ds(part * 256, 256)
                v = recv1[update, pl.ds(k * count + part * 32, 32)].astype(F32).reshape(8, 4, 16, 128)
                parts = swap_blocks([v[:, q] for q in range(4)])
                for side in range(2):
                    rows = jnp.stack([p[:, side * 8 : side * 8 + 8] for p in parts], axis=1)
                    rows = rows.reshape(256, 128)
                    if side == 0 and update == 1:
                        rows = rows.T
                    rows = rows.astype(BF16)
                    if side == 0 and update == 1:
                        left[k, :, at] = rows
                    elif side == 0:
                        left[k, at, :] = rows
                    else:
                        right[core, k, at, :] = rows
            part = right.at[core, k]
            pltpu.make_async_remote_copy(
                src_ref=part, dst_ref=part, send_sem=semxs.at[update], recv_sem=semxr.at[update],
                device_id=sibling, device_id_type=MESH,
            ).start()

        if update == 0:

            def each(i, carry, arrive=arrive):
                arrive(jnp.where(i == 0, 2, jnp.where(i == 3, 0, 2 * i - 1)))
                return carry

            lax.fori_loop(0, 4, each, 0)
        else:
            ways = lax.rem(x + 4 - core * 2, 4)
            other = lax.rem(ways + 3, 4)
            even, odd = jnp.where(lax.rem(ways, 2) == 0, ways, other), jnp.where(lax.rem(ways, 2) == 0, other, ways)
            arrive(jnp.where(even == 2, even, odd))
            arrive(jnp.where(even == 2, odd, even))
        own_back = y == core
        way = lax.rem(core * 2 + 4 - x, 4)
        own_far = (way == 2) | (way == 1)
        own_odd = jnp.where(lax.rem(way, 2) == 1, way, lax.rem(way + 1, 4))

        def block_of(i, own_far=own_far, own_odd=own_odd):
            first = jnp.where(own_far, 2, own_odd)
            second = jnp.where(own_far, own_odd, 2)
            dx = jnp.where(i == 0, first, jnp.where(i == 1, second, jnp.where(i == 2, 4 - own_odd, 0)))
            return lax.rem(x + dx, 4)

        def back_sends(i, rest, update=update, block_of=block_of, own_back=own_back):
            k = block_of(i)

            def send(col, b):
                pltpu.make_async_remote_copy(
                    src_ref=send2.at[update, col * 8 + b],
                    dst_ref=recv2.at[update, me],
                    send_sem=sem2s.at[update],
                    recv_sem=sem2r.at[update],
                    device_id=(core * 8 + b, col),
                    device_id_type=MESH,
                ).start()

            odd = lax.rem(rest + z, 2) == 1
            for h in (1 - yh, yh):
                for way, dz in enumerate(ALONG_Z):
                    b = lax.rem(z + jnp.where(odd, dz[1], dz[0]), 8)
                    send(k * 4 + h * 2 + 1 - core, b)
                    if way < 3 or h is not yh:
                        send(k * 4 + h * 2 + core, b)
                        continue
                    here = (i == 3) & own_back & jnp.logical_not(odd)

                    @pl.when(jnp.logical_not(here))
                    def _(h=h, b=b):
                        send(k * 4 + h * 2 + core, b)

                    @pl.when(here)
                    def _():
                        pltpu.make_async_copy(
                            send2.at[update, c * 8 + z], recv2.at[update, me], sem2r.at[update]
                        ).start()

        def back(i, carry, update=update, left=left, right=right, block_of=block_of, back_sends=back_sends):
            k = block_of(i)
            if update == 0:
                some = pl.ds(pl.multiple_of(lax.rem(k, 2) * 128, 128), 128)
                lhs = jnp.concatenate([left[q] for q in range(4)], axis=1)
                rhs = jnp.concatenate([right[k // 2, q, some, :] for q in range(4)], axis=1)
            else:
                lhs = jnp.concatenate([left[q] for q in range(2)], axis=0)
                rhs = right[k // 2, lax.rem(k, 2)]
            for rest in range(2):
                rows = lhs.reshape(4, 2, 32, 512)[:, rest].reshape(128, 512)
                v = lax.dot_general(rows, rhs, (((1,), (1 - update,)), ((), ())), preferred_element_type=F32)
                v = v.reshape(4, 4, 8, 128)
                parts = swap_blocks([v[:, u] for u in range(4)])
                for q in range(4):
                    for m in range(4):
                        send2[update, (k * 4 + q) * 8 + m * 2 + rest] = parts[q][m].astype(BF16)
                back_sends(i, rest)
            return carry

        back(0, 0)
        theirs = right.at[1 - core]
        pltpu.make_async_copy(theirs, theirs, semxr.at[update]).wait()
        lax.fori_loop(1, 4, back, 0)
        pltpu.make_async_copy(recv2.at[update], recv2.at[update], sem2r.at[update]).wait()

        tiles = jnp.swapaxes(recv2[update].astype(F32), 0, 1)
        for t in range(8):
            v = tiles[t]
            centred = v - jnp.mean(v, axis=0, keepdims=True)
            variance = jnp.mean(centred * centred, axis=0, keepdims=True)
            v = (centred * lax.rsqrt(variance + EPS)).astype(BF16)
            term = lax.dot_general(v, wout[update], (((0,), (0,)), ((), ())), preferred_element_type=F32)
            at = pl.ds(t * 128, 128)
            new = zp[t].reshape(128, 128).astype(F32) + gate[at, :] * term
            if update == 0:
                new = new.astype(BF16)
                zp[t] = new.reshape(4, 32, 128)
                normalize_rows(t, new.astype(F32))
            else:
                for u in range(4):
                    out_ref[u * 8 + t] = new[u * 32 : u * 32 + 32].astype(BF16)

        mine = right.at[core]
        pltpu.make_async_copy(mine, mine, semxs.at[update]).wait()
        for sent, sem, all_remote, count in (
            (send1, sem1s, jnp.logical_not(own), 128),
            (send2, sem2s, jnp.logical_not(own_back), 128),
        ):

            @pl.when(all_remote)
            def _(update=update, sent=sent, sem=sem):
                pltpu.make_async_copy(sent.at[update], sent.at[update], sem.at[update]).wait()

            @pl.when(jnp.logical_not(all_remote))
            def _(update=update, sent=sent, sem=sem, count=count):
                gone = sent.at[update, pl.ds(0, count - 1)]
                pltpu.make_async_copy(gone, gone, sem.at[update]).wait()


def per_device(pair_rep, residue_mask, input_weights, gate_weights, output_weights):
    vmem = pl.BlockSpec(memory_space=pltpu.VMEM)
    anywhere = pl.BlockSpec(memory_space=pl.ANY)
    dma = pltpu.SemaphoreType.DMA((2,))
    out = pl.pallas_call(
        kernel,
        out_shape=jax.ShapeDtypeStruct((32, 32, 128), BF16),
        in_specs=[anywhere] * 5,
        out_specs=vmem,
        scratch_shapes=[
            pltpu.VMEM((8, 4, 32, 128), BF16),
            pltpu.VMEM((1, 512), jnp.int32),
            pltpu.VMEM((2, 128, 512), BF16),
            pltpu.VMEM((2, 128, 128), BF16),
            pltpu.VMEM((2, 128, 128), BF16),
            pltpu.VMEM((1024, 128), BF16),
            pltpu.VMEM((2, 4, 128, 128), BF16),
            pltpu.VMEM((8, 128), F32),
            pltpu.VMEM((1024, 128), F32),
            pltpu.VMEM((2, 128, 16, 128), BF16),
            pltpu.VMEM((2, 128, 16, 128), BF16),
            pltpu.VMEM((4, 256, 128), BF16),
            pltpu.VMEM((2, 4, 256, 128), BF16),
            pltpu.VMEM((2, 128, 512), BF16),
            pltpu.VMEM((2, 2, 512, 128), BF16),
            pltpu.VMEM((2, 128, 8, 128), BF16),
            pltpu.VMEM((2, 128, 8, 128), BF16),
            pltpu.SemaphoreType.DMA((12,)),
            dma, pltpu.SemaphoreType.DMA((2, 4)), dma, dma, dma, dma,
            pltpu.SemaphoreType.REGULAR((8,)),
        ],
        compiler_params=pltpu.CompilerParams(
            collective_id=0, has_side_effects=True, vmem_limit_bytes=32 * 1024 * 1024
        ),
        name="triangles",
    )(
        pltpu.with_memory_space_constraint(pair_rep.reshape(4, 8, 32, 128), pltpu.HBM),
        pltpu.with_memory_space_constraint(residue_mask.reshape(1, 512), pltpu.HBM),
        pltpu.with_memory_space_constraint(input_weights, pltpu.HBM),
        pltpu.with_memory_space_constraint(gate_weights, pltpu.HBM),
        pltpu.with_memory_space_constraint(output_weights, pltpu.HBM),
    )
    return out


def solution(mesh):
    placed = (P("row", "col", None), P(), P(), P(), P())
    return jax.shard_map(
        per_device, mesh=mesh, in_specs=placed, out_specs=P("row", "col", None), check_vma=False
    )
```

```python
import functools

import jax
import jax.numpy as jnp
from jax import lax
from jax.experimental import pallas as pl
from jax.experimental.pallas import tpu as pltpu
from jax.sharding import PartitionSpec as P

EPS = 1e-05
MESH = pl.DeviceIdType.MESH
F32 = jnp.float32
BF16 = jnp.bfloat16


def sigmoid(x):
    return 0.5 * jnp.tanh(0.5 * x) + 0.5


def swap_blocks(parts):
    group = lax.broadcasted_iota(jnp.int32, parts[0].shape, parts[0].ndim - 1) // 32
    axis = parts[0].ndim - 1
    high = group >= 2
    odd = lax.rem(group, 2) == 1

    def far(a, b):
        c = pltpu.roll(jnp.where(high, a, b), 64, axis)
        return jnp.where(high, c, a), jnp.where(high, b, c)

    def near(a, b):
        c = jnp.where(odd, a, b)
        return jnp.where(odd, pltpu.roll(c, 32, axis), a), jnp.where(odd, b, pltpu.roll(c, 96, axis))

    p0, p2 = far(parts[0], parts[2])
    p1, p3 = far(parts[1], parts[3])
    p0, p1 = near(p0, p1)
    p2, p3 = near(p2, p3)
    return p0, p1, p2, p3


def far_first(step):
    pair, second = step // 2, lax.rem(step, 2)
    middle = (pair == 1) | (pair == 2)
    dx = jnp.where(middle, 1 + 2 * second, jnp.where(pair == 0, 2, 0))
    return dx, jnp.where(middle, 2 - pair, 1 - second)


ALONG_Z = ((4, 3), (2, 5), (6, 1), (0, 7))


def kernel(
    z_hbm, mask_hbm, win_hbm, wgate_hbm, wout_hbm, out_ref,
    zp, mask_ref, win, wgate, wout, normed, wt, mask8, gate,
    send1, recv1, left0, right0, left1, right1, send2, recv2,
    load, sem1s, sem1r, semxs, semxr, sem2s, sem2r, ready,
):
    r, c = lax.axis_index("row"), lax.axis_index("col")
    cc, core = c // 2, lax.rem(c, 2)
    y, z = r // 8, lax.rem(r, 8)
    x, yh = cc // 2, lax.rem(cc, 2)
    me = cc * 16 + r
    sibling = (r, cc * 2 + 1 - core)

    loads = [pltpu.make_async_copy(z_hbm.at[:, t], zp.at[t], load.at[t]) for t in range(8)]
    loads.append(pltpu.make_async_copy(win_hbm, win, load.at[8]))
    loads.append(pltpu.make_async_copy(wgate_hbm, wgate, load.at[9]))
    loads.append(pltpu.make_async_copy(wout_hbm, wout, load.at[10]))
    loads.append(pltpu.make_async_copy(mask_hbm, mask_ref, load.at[11]))
    for one in loads:
        one.start()

    barrier = pltpu.get_barrier_semaphore()

    for dz in (4, 3, 5, 2, 6, 1, 7, 0):
        row = core * 8 + lax.rem(z + dz, 8)
        for k in range(2):
            far = lax.rem(x + 2, 4) * 4 + (1 - yh) * 2 + k
            pl.semaphore_signal(barrier, inc=1, device_id=(row, far), device_id_type=MESH)

    @pl.loop(1, 8)
    def _(t):
        peer = lax.rem(cc + t, 8) * 2 + core
        pl.semaphore_signal(barrier, inc=1, device_id=(r, peer), device_id_type=MESH)

    n8 = lax.broadcasted_iota(jnp.int32, (8, 512), 1)
    t8 = lax.broadcasted_iota(jnp.int32, (8, 512), 0)
    n = lax.broadcasted_iota(jnp.int32, (512, 128), 0)
    l = lax.broadcasted_iota(jnp.int32, (512, 128), 1)
    pick_row = jnp.where(n // 8 == 4 * r + l // 32, 1.0, 0.0).astype(BF16)
    pick_col = jnp.where(n == 32 * c + lax.rem(l, 32), 1.0, 0.0).astype(BF16)
    loads[11].wait()
    valid = jnp.broadcast_to(mask_ref[...].astype(F32), (8, 512))
    rows = jnp.where(lax.rem(n8, 8) == t8, valid, 0.0).astype(BF16)
    mask8[...] = jnp.dot(rows, pick_row, preferred_element_type=F32) * jnp.dot(
        valid.astype(BF16), pick_col, preferred_element_type=F32
    )

    def normalize_rows(t, v):
        centred = v - jnp.mean(v, axis=-1, keepdims=True)
        variance = jnp.mean(centred * centred, axis=-1, keepdims=True)
        normed[pl.ds(t * 128, 128), :] = (centred * lax.rsqrt(variance + EPS)).astype(BF16)

    def turn_weights(u):
        for k in range(4):
            wt[u, k] = win[u, :, k * 128 : (k + 1) * 128].astype(F32).T.astype(BF16)

    def serves(step, update):
        if update == 1:
            return far_first(step)
        far = (1 - yh) * 4 + lax.rem(x + 2, 4)
        place = jnp.where(step == 0, far, jnp.where(step - 1 < far, step - 1, step))
        return lax.rem(lax.rem(place, 4) + 4 - x, 4), lax.rem(place // 4 + yh, 2)

    def project(step, update):
        dx, dh = serves(step, update)
        chip = lax.rem(x + dx, 4) * 2 + lax.rem(yh + dh, 2)
        at = pl.ds(pl.multiple_of(chip * 16, 16), 16)
        w = jnp.concatenate([wt[update, k, at, :] for k in range(4)], axis=0)
        p = lax.dot_general(w, normed[...], (((1,), (1,)), ((), ())), preferred_element_type=F32)
        both = []
        for k in (0, 32):
            side = sigmoid(p[k + 16 : k + 32]) * p[k : k + 16]
            tiles = jnp.stack([side[:, t * 128 : (t + 1) * 128] for t in range(8)], axis=0)
            both.append(jnp.swapaxes(tiles, 0, 1) * mask8[...][None])
        send1[update, at] = jnp.concatenate(both, axis=1).astype(BF16)

    for t in range(8):
        loads[t].wait()
        normalize_rows(t, zp[t].reshape(128, 128).astype(F32))
    loads[8].wait()
    turn_weights(0)

    for update in range(2):
        half = y if update == 0 else c // 8
        corner = lax.rem(c, 4)
        slot = x * 32 + z * 4 + corner if update == 0 else lax.rem(x, 2) * 64 + r * 4 + corner
        own = half == core

        def spread(step, update=update, half=half, own=own, slot=slot):
            dx, dh = serves(step, update)
            chip = lax.rem(x + dx, 4) * 2 + lax.rem(yh + dh, 2)

            def send(row):
                pltpu.make_async_remote_copy(
                    src_ref=send1.at[update, chip * 16 + row],
                    dst_ref=recv1.at[update, slot],
                    send_sem=sem1s.at[update],
                    recv_sem=sem1r.at[update, dx],
                    device_id=(row, chip * 2 + half),
                    device_id_type=MESH,
                ).start()

            near = lax.rem(y + dh, 2)
            for parity, line in ((0, 1 - near), (0, near), (1, 1 - near), (1, near)):
                odd = lax.rem(parity + line + z + chip // 2 + chip, 2) == 1
                for way, dz in enumerate(ALONG_Z):
                    row = line * 8 + lax.rem(z + jnp.where(odd, dz[1], dz[0]), 8)
                    if way < 3 or line is not near:
                        send(row)
                        continue
                    here = (dx == 0) & (dh == 0) & own & jnp.logical_not(odd)

                    @pl.when(jnp.logical_not(here))
                    def _(row=row):
                        send(row)

                    @pl.when(here)
                    def _():
                        pltpu.make_async_copy(
                            send1.at[update, me], recv1.at[update, slot], sem1r.at[update, dx]
                        ).start()

        if update == 0:
            project(0, 0)
            pl.semaphore_wait(barrier, 23)

            place = (1 - yh) * 4 + lax.rem(x + 2, 4)

            @pl.loop(1, 8)
            def _(t, place=place):
                peer = lax.rem(cc + t, 8) * 2 + core
                pl.semaphore_signal(ready.at[place], inc=1, device_id=(r, peer), device_id_type=MESH)

            spread(0)

            @pl.loop(1, 8)
            def _(step, spread=spread):
                project(step, 0)
                dx, dh = serves(step, 0)
                place = lax.rem(yh + dh, 2) * 4 + lax.rem(x + dx, 4)
                pl.semaphore_wait(ready.at[place], 1)
                spread(step)

        else:

            @pl.loop(0, 8)
            def _(step, spread=spread):
                project(step, 1)
                spread(step)

        if update == 0:
            turn_weights(1)
            loads[9].wait()
            loads[10].wait()

        @pl.loop(0, 4)
        def _(i, update=update):
            at = pl.ds(pl.multiple_of(i * 256, 256), 256)
            gate[at, :] = sigmoid(jnp.dot(normed[at, :], wgate[update], preferred_element_type=F32))

        left, right = (left0, right0) if update == 0 else (left1, right1)
        columns = 4 if update == 0 else 2
        count = 128 // columns

        def arrive(dx, update=update, left=left, right=right, columns=columns, count=count):
            k = lax.rem(x + 4 - dx, columns)
            got = recv1.at[update, pl.ds(0, count)]
            pltpu.make_async_copy(got, got, sem1r.at[update, dx]).wait()
            for part in range(count // 32):
                at = pl.ds(part * 256, 256)
                v = recv1[update, pl.ds(k * count + part * 32, 32)].astype(F32).reshape(8, 4, 16, 128)
                parts = swap_blocks([v[:, q] for q in range(4)])
                for side in range(2):
                    rows = jnp.stack([p[:, side * 8 : side * 8 + 8] for p in parts], axis=1)
                    rows = rows.reshape(256, 128)
                    if side == 0 and update == 1:
                        rows = rows.T
                    rows = rows.astype(BF16)
                    if side == 0 and update == 1:
                        left[k, :, at] = rows
                    elif side == 0:
                        left[k, at, :] = rows
                    else:
                        right[core, k, at, :] = rows
            part = right.at[core, k]
            pltpu.make_async_remote_copy(
                src_ref=part, dst_ref=part, send_sem=semxs.at[update], recv_sem=semxr.at[update],
                device_id=sibling, device_id_type=MESH,
            ).start()

        if update == 0:

            def each(i, carry, arrive=arrive):
                arrive(jnp.where(i == 0, 2, jnp.where(i == 3, 0, 2 * i - 1)))
                return carry

            lax.fori_loop(0, 4, each, 0)
        else:
            ways = lax.rem(x + 4 - core * 2, 4)
            other = lax.rem(ways + 3, 4)
            even, odd = jnp.where(lax.rem(ways, 2) == 0, ways, other), jnp.where(lax.rem(ways, 2) == 0, other, ways)
            arrive(jnp.where(even == 2, even, odd))
            arrive(jnp.where(even == 2, odd, even))
        own_back = y == core
        way = lax.rem(core * 2 + 4 - x, 4)
        own_far = (way == 2) | (way == 1)
        own_odd = jnp.where(lax.rem(way, 2) == 1, way, lax.rem(way + 1, 4))

        def block_of(i, own_far=own_far, own_odd=own_odd):
            first = jnp.where(own_far, 2, own_odd)
            second = jnp.where(own_far, own_odd, 2)
            dx = jnp.where(i == 0, first, jnp.where(i == 1, second, jnp.where(i == 2, 4 - own_odd, 0)))
            return lax.rem(x + dx, 4)

        def back_sends(i, rest, update=update, block_of=block_of, own_back=own_back):
            k = block_of(i)

            def send(col, b):
                pltpu.make_async_remote_copy(
                    src_ref=send2.at[update, col * 8 + b],
                    dst_ref=recv2.at[update, me],
                    send_sem=sem2s.at[update],
                    recv_sem=sem2r.at[update],
                    device_id=(core * 8 + b, col),
                    device_id_type=MESH,
                ).start()

            odd = lax.rem(rest + z, 2) == 1
            for h in (1 - yh, yh):
                for way, dz in enumerate(ALONG_Z):
                    b = lax.rem(z + jnp.where(odd, dz[1], dz[0]), 8)
                    send(k * 4 + h * 2 + 1 - core, b)
                    if way < 3 or h is not yh:
                        send(k * 4 + h * 2 + core, b)
                        continue
                    here = (i == 3) & own_back & jnp.logical_not(odd)

                    @pl.when(jnp.logical_not(here))
                    def _(h=h, b=b):
                        send(k * 4 + h * 2 + core, b)

                    @pl.when(here)
                    def _():
                        pltpu.make_async_copy(
                            send2.at[update, c * 8 + z], recv2.at[update, me], sem2r.at[update]
                        ).start()

        def back(i, carry, update=update, left=left, right=right, block_of=block_of, back_sends=back_sends):
            k = block_of(i)
            if update == 0:
                some = pl.ds(pl.multiple_of(lax.rem(k, 2) * 128, 128), 128)
                lhs = jnp.concatenate([left[q] for q in range(4)], axis=1)
                rhs = jnp.concatenate([right[k // 2, q, some, :] for q in range(4)], axis=1)
            else:
                lhs = jnp.concatenate([left[q] for q in range(2)], axis=0)
                rhs = right[k // 2, lax.rem(k, 2)]
            for rest in range(2):
                rows = lhs.reshape(4, 2, 32, 512)[:, rest].reshape(128, 512)
                v = lax.dot_general(rows, rhs, (((1,), (1 - update,)), ((), ())), preferred_element_type=F32)
                v = v.reshape(4, 4, 8, 128)
                parts = swap_blocks([v[:, u] for u in range(4)])
                for q in range(4):
                    for m in range(4):
                        send2[update, (k * 4 + q) * 8 + m * 2 + rest] = parts[q][m].astype(BF16)
                back_sends(i, rest)
            return carry

        back(0, 0)
        theirs = right.at[1 - core]
        pltpu.make_async_copy(theirs, theirs, semxr.at[update]).wait()
        lax.fori_loop(1, 4, back, 0)
        pltpu.make_async_copy(recv2.at[update], recv2.at[update], sem2r.at[update]).wait()

        tiles = jnp.swapaxes(recv2[update].astype(F32), 0, 1)
        for t in range(8):
            v = tiles[t]
            centred = v - jnp.mean(v, axis=0, keepdims=True)
            variance = jnp.mean(centred * centred, axis=0, keepdims=True)
            v = (centred * lax.rsqrt(variance + EPS)).astype(BF16)
            term = lax.dot_general(v, wout[update], (((0,), (0,)), ((), ())), preferred_element_type=F32)
            at = pl.ds(t * 128, 128)
            new = zp[t].reshape(128, 128).astype(F32) + gate[at, :] * term
            if update == 0:
                new = new.astype(BF16)
                zp[t] = new.reshape(4, 32, 128)
                normalize_rows(t, new.astype(F32))
            else:
                for u in range(4):
                    out_ref[u * 8 + t] = new[u * 32 : u * 32 + 32].astype(BF16)

        mine = right.at[core]
        pltpu.make_async_copy(mine, mine, semxs.at[update]).wait()
        for sent, sem, all_remote, count in (
            (send1, sem1s, jnp.logical_not(own), 128),
            (send2, sem2s, jnp.logical_not(own_back), 128),
        ):

            @pl.when(all_remote)
            def _(update=update, sent=sent, sem=sem):
                pltpu.make_async_copy(sent.at[update], sent.at[update], sem.at[update]).wait()

            @pl.when(jnp.logical_not(all_remote))
            def _(update=update, sent=sent, sem=sem, count=count):
                gone = sent.at[update, pl.ds(0, count - 1)]
                pltpu.make_async_copy(gone, gone, sem.at[update]).wait()


def per_device(pair_rep, residue_mask, input_weights, gate_weights, output_weights):
    vmem = pl.BlockSpec(memory_space=pltpu.VMEM)
    anywhere = pl.BlockSpec(memory_space=pl.ANY)
    dma = pltpu.SemaphoreType.DMA((2,))
    out = pl.pallas_call(
        kernel,
        out_shape=jax.ShapeDtypeStruct((32, 32, 128), BF16),
        in_specs=[anywhere] * 5,
        out_specs=vmem,
        scratch_shapes=[
            pltpu.VMEM((8, 4, 32, 128), BF16),
            pltpu.VMEM((1, 512), jnp.int32),
            pltpu.VMEM((2, 128, 512), BF16),
            pltpu.VMEM((2, 128, 128), BF16),
            pltpu.VMEM((2, 128, 128), BF16),
            pltpu.VMEM((1024, 128), BF16),
            pltpu.VMEM((2, 4, 128, 128), BF16),
            pltpu.VMEM((8, 128), F32),
            pltpu.VMEM((1024, 128), F32),
            pltpu.VMEM((2, 128, 16, 128), BF16),
            pltpu.VMEM((2, 128, 16, 128), BF16),
            pltpu.VMEM((4, 256, 128), BF16),
            pltpu.VMEM((2, 4, 256, 128), BF16),
            pltpu.VMEM((2, 128, 512), BF16),
            pltpu.VMEM((2, 2, 512, 128), BF16),
            pltpu.VMEM((2, 128, 8, 128), BF16),
            pltpu.VMEM((2, 128, 8, 128), BF16),
            pltpu.SemaphoreType.DMA((12,)),
            dma, pltpu.SemaphoreType.DMA((2, 4)), dma, dma, dma, dma,
            pltpu.SemaphoreType.REGULAR((8,)),
        ],
        compiler_params=pltpu.CompilerParams(
            collective_id=0, has_side_effects=True, vmem_limit_bytes=32 * 1024 * 1024
        ),
        name="triangles",
    )(
        pltpu.with_memory_space_constraint(pair_rep.reshape(4, 8, 32, 128), pltpu.HBM),
        pltpu.with_memory_space_constraint(residue_mask.reshape(1, 512), pltpu.HBM),
        pltpu.with_memory_space_constraint(input_weights, pltpu.HBM),
        pltpu.with_memory_space_constraint(gate_weights, pltpu.HBM),
        pltpu.with_memory_space_constraint(output_weights, pltpu.HBM),
    )
    return out


def solution(mesh):
    placed = (P("row", "col", None), P(), P(), P(), P())
    return jax.shard_map(
        per_device, mesh=mesh, in_specs=placed, out_specs=P("row", "col", None), check_vma=False
    )
```
